512 devices in a mesh: blk: 16 (over y, z_hi), grp: 32 (over z_lo, x, core).
Axes of the slice: x: 4, y: 8, z: 8 (z_hi: 2, z_lo: 4; z = z_hi * 4 + z_lo), core: 2. Of those that a mesh axis runs over, the one named last changes fastest.
Arguments:
- images: bfloat16 [12288, 1152], P(('blk', 'grp')), may hold values from -0.19921875 to 0.19921875
- texts: bfloat16 [16384, 1152], P(('blk', 'grp')), may hold values from -0.19921875 to 0.19921875
- image_ids: int32 [12288], replicated, may hold values from 0 to 12287, each once
- text_ids: int32 [16384], replicated, may hold values from 0 to 12287
- log_scale: float32 [1], replicated, may hold values from 1.6 to 2.4
- bias: float32 [1], replicated, may hold values from -8 to -4
Outputs:
- image_grad: float32 [12288, 1152], P(('blk', 'grp'))
- text_grad: float32 [16384, 1152], P(('blk', 'grp'))
- loss: float32 [1], replicated
- scale_grad: float32 [1], replicated
- bias_grad: float32 [1], replicated
The draws below stay inside these ranges and needn't reach their ends.
Inputs may be any that keep to these rules, and one draw needn't show every extreme that they name: `image_ids`: each pair id appears on exactly one image.
All inputs are finite; a program needn't handle non-finite values.
Results may differ from the reference program's by a relative error of at most 0.00075.
The reference program's roundings to bfloat16 on the way (of `slopeb`) count: a program that leaves them out, or rounds other values in their place, can miss the bound.
Values may be sent and summed in bfloat16 or wider, within the bound.
No kernel may reach another device: no remote copies, remote signals or barrier semaphores. Data moves between devices by JAX's collectives and lax.ppermute only.
A program may use at most 64 MiB of HBM per device.

```python
import jax
import jax.numpy as jnp
from jax import lax

D = 1152
IMG_DEV = 24
IMAGES = 12288
TEXTS = 16384
N_BLK = 16
N_GRP = 32


def place_ends(entries, own_key, low, largest):
    spot = [jax.random.randint(jax.random.fold_in(own_key, axis), (), 0, length) for axis, length in enumerate(entries.shape)]
    widest = entries.shape.index(max(entries.shape))
    next_to = spot[:widest] + [(spot[widest] + 1) % entries.shape[widest]] + spot[widest + 1:]
    return entries.at[tuple(spot)].set(low).at[tuple(next_to)].set(largest)


def shard_levels(own_key, extent, cuts, smallest, high):
    level = 1.0
    for dim, parts in cuts:
        draws = jax.random.uniform(jax.random.fold_in(jax.random.fold_in(own_key, 6), dim), (parts,), jnp.float32, smallest / len(cuts), high / len(cuts))
        level = level * jnp.repeat(jnp.exp(draws), extent[dim] // parts).reshape((-1,) + (1,) * (len(extent) - 1 - dim))
    return level


def noise(rng, dims, spread, bound, split=(), held_as=jnp.bfloat16):
    loudness = shard_levels(rng, dims, split, -0.22, 0.18) if split else 1.0
    values = jax.random.normal(rng, dims, jnp.float32) * spread * loudness
    return jnp.minimum(jnp.maximum(values, -bound), bound).astype(held_as)


def setup_inputs(seed: int = 0) -> dict:
    key_of = jax.random.split(jax.random.key(seed), 7)
    images = noise(key_of[0], (IMAGES, D), 0.03, 0.19921875, ((0, 512),))
    texts = noise(key_of[1], (TEXTS, D), 0.03, 0.19921875, ((0, 512),))
    image_ids = jax.random.permutation(key_of[2], IMAGES).astype(jnp.int32)
    text_ids = place_ends(jax.random.randint(key_of[3], (TEXTS,), 0, IMAGES), jax.random.fold_in(key_of[3], 1), 0, IMAGES - 1).astype(jnp.int32)
    log_scale = jnp.clip(jax.random.uniform(key_of[4], (1,), jnp.float32, 1.6, 2.4), 1.6, 2.4)
    bias = jnp.clip(jax.random.uniform(key_of[5], (1,), jnp.float32, -8.0, -4.0), -8.0, -4.0)
    return dict(images=images, texts=texts, image_ids=image_ids, text_ids=text_ids, log_scale=log_scale, bias=bias)


def normalize(rows):
    values = rows.astype(jnp.float32)
    radius = jnp.sqrt(lax.optimization_barrier(jnp.sum(values * values, -1, keepdims=True)) + 1e-06)
    unit = values / radius
    return (unit, radius, unit.astype(jnp.bfloat16))

def unnormalize(unit, radius, grad):
    return (grad - unit * lax.optimization_barrier(jnp.sum(unit * grad, -1, keepdims=True))) / radius

def pair_terms(left, left_ids, right, right_ids, scale, shift):
    dots = jnp.dot(left, right.T, preferred_element_type=jnp.float32)
    logits = scale * dots + shift
    sign = jnp.where(left_ids[:, None] == right_ids[None, :], 1.0, -1.0).astype(jnp.float32)
    margin = sign * logits
    objective = jnp.sum(jax.nn.softplus(-margin))
    slope = -sign * jax.nn.sigmoid(-margin)
    return (slope, objective, jnp.sum(slope * dots), jnp.sum(slope))

def reference(images, texts, image_ids, text_ids, log_scale, bias):
    scale = jnp.exp(log_scale[0])
    shift = bias[0]
    ux, rx, uxb = normalize(images)
    uy, ry, uyb = normalize(texts)
    rows = IMG_DEV * N_GRP
    blocks = uxb.reshape(N_BLK, rows, D)
    block_ids = image_ids.reshape(N_BLK, rows)

    def visit(carry, item):
        tgrad, objective, dot_sum, slope_sum = carry
        block, ids = item
        slope, obj, s_dot, s_slope = pair_terms(block, ids, uyb, text_ids, scale, shift)
        slopeb = slope.astype(jnp.bfloat16)
        igrad = scale * jnp.dot(slopeb, uyb, preferred_element_type=jnp.float32)
        tgrad = tgrad + scale * jnp.dot(slopeb.T, block, preferred_element_type=jnp.float32)
        return ((tgrad, objective + obj, dot_sum + s_dot, slope_sum + s_slope), igrad)
    zero = jnp.zeros((), jnp.float32)
    init = (jnp.zeros((TEXTS, D), jnp.float32), zero, zero, zero)
    (tgrad, objective, dot_sum, slope_sum), igrads = lax.scan(visit, init, (blocks, block_ids))
    image_grad = unnormalize(ux, rx, igrads.reshape(IMAGES, D))
    text_grad = unnormalize(uy, ry, tgrad)
    loss = (objective / TEXTS).reshape(1)
    scale_grad = (scale * dot_sum / TEXTS).reshape(1)
    bias_grad = (slope_sum / TEXTS).reshape(1)
    return (image_grad, text_grad, loss, scale_grad, bias_grad)
```

```python
import jax
import jax.numpy as jnp
from jax import lax
from jax.sharding import Mesh, PartitionSpec as P

AXES = ("y", "zh", "zl", "x", "core")
SIZES = (8, 2, 4, 4, 2)
Z = ("zh", "zl")


def normalize(rows):
    values = rows.astype(jnp.float32)
    radius = jnp.sqrt(jnp.sum(values * values, -1, keepdims=True) + 1e-06)
    unit = values / radius
    return (unit, radius, unit.astype(jnp.bfloat16))


def unnormalize(unit, radius, grad):
    return (grad - unit * jnp.sum(unit * grad, -1, keepdims=True)) / radius


def swap(value, axis):
    return lax.all_to_all(value, axis, 0, 0, tiled=False)


def spread(block, axis):
    count = lax.axis_size(axis)
    return swap(jnp.broadcast_to(block[None], (count,) + block.shape), axis)


def body(images, texts, image_ids, text_ids, log_scale, bias):
    width = images.shape[1]
    img_rows = images.shape[0]
    txt_rows = texts.shape[0]
    y, x, core = (lax.axis_index(a) for a in ("y", "x", "core"))
    z = lax.axis_index(Z)
    scale = jnp.exp(log_scale[0])
    shift = bias[0]
    uy, ry, uyb = normalize(texts)
    ux, rx, uxb = normalize(images)

    cols = lax.all_gather(uyb, Z + ("core",), axis=0, tiled=True)
    cols = cols.reshape(8, 2, txt_rows, width).transpose(1, 0, 2, 3).reshape(-1, width)
    rows = spread(uxb, "y").reshape(-1, width)
    rows = spread(rows, "x").reshape(-1, width)

    col_ids = text_ids.reshape(8, 8, 4, 2, txt_rows)
    col_ids = lax.dynamic_index_in_dim(col_ids, y, 0, keepdims=False)
    col_ids = lax.dynamic_index_in_dim(col_ids, x, 1, keepdims=False)
    col_ids = col_ids.transpose(1, 0, 2).reshape(-1)
    row_ids = image_ids.reshape(8, 8, 4, 2, img_rows)
    row_ids = lax.dynamic_index_in_dim(row_ids, z, 1, keepdims=False)
    row_ids = lax.dynamic_index_in_dim(row_ids, core, 2, keepdims=False)
    row_ids = row_ids.transpose(1, 0, 2).reshape(-1)

    dots = jnp.dot(rows, cols.T, preferred_element_type=jnp.float32)
    logits = scale * dots + shift
    match = row_ids[:, None] == col_ids[None, :]
    against = jnp.where(match, -logits, logits)
    decay = jnp.exp(-jnp.abs(against))
    objective = jnp.sum(jnp.maximum(against, 0.0) + jnp.log1p(decay))
    weight = jnp.where(against >= 0.0, 1.0, decay) / (1.0 + decay)
    slope = jnp.where(match, -weight, weight)
    stats = jnp.stack([objective, jnp.sum(slope * dots), jnp.sum(slope)])
    slopeb = slope.astype(jnp.bfloat16)

    dcols = jnp.dot(slopeb.T, rows, preferred_element_type=jnp.float32)
    dcols = jnp.sum(swap(dcols.reshape(2, -1, width), "core"), 0)
    text_accum = lax.psum_scatter(dcols, Z, scatter_dimension=0, tiled=True)

    drows = jnp.dot(slopeb, cols, preferred_element_type=jnp.float32)
    drows = (drows * 64.0).astype(jnp.float16).reshape(4, -1, width)
    drows = jnp.sum(swap(drows, "x").astype(jnp.float32), 0)
    drows = (drows * 0.25).astype(jnp.float16).reshape(8, -1, width)
    image_accum = jnp.sum(swap(drows, "y").astype(jnp.float32), 0) * 0.0625

    for axis in ("core", Z, "x", "y"):
        stats = lax.psum(stats, axis)
    total_texts = txt_rows * 512
    image_grad = unnormalize(ux, rx, scale * image_accum)
    text_grad = unnormalize(uy, ry, scale * text_accum)
    loss = (stats[0] / total_texts).reshape(1)
    scale_grad = (scale * stats[1] / total_texts).reshape(1)
    bias_grad = (stats[2] / total_texts).reshape(1)
    return (image_grad, text_grad, loss, scale_grad, bias_grad)


def solution(mesh):
    fine = Mesh(mesh.devices.reshape(SIZES), AXES)
    split = P(AXES, None)
    return jax.shard_map(
        body,
        mesh=fine,
        in_specs=(split, split, P(), P(), P(), P()),
        out_specs=(split, split, P(), P(), P()),
        check_vma=False,
    )
```

```python
import jax
import jax.numpy as jnp
from jax import lax
from jax.sharding import Mesh, PartitionSpec as P

AXES = ("y", "zh", "zl", "x", "core")
SIZES = (8, 2, 4, 4, 2)
Z = ("zh", "zl")
UNIT = 16384.0


def normalize(rows):
    values = rows.astype(jnp.float32)
    radius = jnp.sqrt(jnp.sum(values * values, -1, keepdims=True) + 1e-06)
    unit = values / radius
    return (unit, radius, lax.reduce_precision(unit, 8, 7))


def unnormalize(unit, radius, grad):
    return (grad - unit * jnp.sum(unit * grad, -1, keepdims=True)) / radius


def swap(value, axis):
    return lax.all_to_all(value, axis, 0, 0, tiled=False)


def shifted(value, axis, steps):
    count = lax.axis_size(axis)
    return lax.ppermute(value, axis, [(i, (i + steps) % count) for i in range(count)])


def spread(block, axis):
    count = lax.axis_size(axis)
    return swap(jnp.broadcast_to(block[None], (count,) + block.shape), axis)


def body(images, texts, image_ids, text_ids, log_scale, bias):
    width = images.shape[1]
    img_rows = images.shape[0]
    txt_rows = texts.shape[0]
    y, x, core = (lax.axis_index(a) for a in ("y", "x", "core"))
    z = lax.axis_index(Z)
    scale = jnp.exp(log_scale[0])
    shift = bias[0]
    ux, rx, uxb = normalize(images)
    uy, ry, uyb = normalize(texts)

    own = spread(uxb.astype(jnp.bfloat16), "y").reshape(-1, width)
    cols = (uyb * UNIT).astype(jnp.float16)
    cols = lax.all_gather(cols, Z + ("core",), axis=0, tiled=True)
    cols = (cols.astype(jnp.float32) * (1 / UNIT)).astype(jnp.bfloat16)
    cols = cols.reshape(8, 2, txt_rows, width)
    cols = jnp.concatenate([cols[:, 0], cols[:, 1]], 0).reshape(-1, width)

    col_ids = text_ids.reshape(8, 8, 4, 2, txt_rows)
    col_ids = lax.dynamic_index_in_dim(col_ids, y, 0, keepdims=False)
    col_ids = lax.dynamic_index_in_dim(col_ids, x, 1, keepdims=False)
    col_ids = col_ids.transpose(1, 0, 2).reshape(-1)
    row_ids = image_ids.reshape(8, 8, 4, 2, img_rows)
    row_ids = lax.dynamic_index_in_dim(row_ids, z, 1, keepdims=False)
    row_ids = lax.dynamic_index_in_dim(row_ids, core, 2, keepdims=False)
    row_ids = row_ids.transpose(1, 0, 2).reshape(4, -1)

    order = (0, 1, 3, 2)
    parts = {k: shifted(own, "x", k) if k else own for k in order}
    slopes, back, stats = {}, {}, jnp.zeros((3,), jnp.float32)
    for k in order:
        ids = lax.dynamic_index_in_dim(row_ids, (x - k) % 4, 0, keepdims=False)
        dots = jnp.dot(parts[k], cols.T, preferred_element_type=jnp.float32)
        logits = scale * dots + shift
        match = ids[:, None] == col_ids[None, :]
        against = jnp.where(match, -logits, logits)
        decay = jnp.exp(-jnp.abs(against))
        objective = jnp.sum(jnp.maximum(against, 0.0) + jnp.log1p(decay))
        weight = jnp.where(against >= 0.0, 1.0, decay) / (1.0 + decay)
        slope = jnp.where(match, -weight, weight)
        stats += jnp.stack([objective, jnp.sum(slope * dots), jnp.sum(slope)])
        slopes[k] = slope.astype(jnp.bfloat16)
        drows = jnp.dot(slopes[k], cols, preferred_element_type=jnp.float32)
        back[k] = shifted((drows * 64.0).astype(jnp.float16), "x", -k) if k else drows * 64.0

    rows = jnp.concatenate([parts[k] for k in order], 0)
    weights = jnp.concatenate([slopes[k] for k in order], 0).reshape(-1, 2, 8 * txt_rows)
    theirs = lax.dynamic_index_in_dim(weights, 1 - core, 1, keepdims=False)
    mine = lax.dynamic_index_in_dim(weights, core, 1, keepdims=False)
    theirs = jnp.dot(theirs.T, rows, preferred_element_type=jnp.float32)
    theirs = shifted(theirs, "core", 1)
    dcols = theirs + jnp.dot(mine.T, rows, preferred_element_type=jnp.float32)
    dcols = (dcols * 32.0).astype(jnp.float16).reshape(8, txt_rows, width)
    text_accum = jnp.sum(swap(dcols, Z).astype(jnp.float32), 0) * (1 / 32.0)

    drows = sum(back[k].astype(jnp.float32) for k in order)
    drows = (drows * 0.25).astype(jnp.float16).reshape(8, -1, width)
    image_accum = jnp.sum(swap(drows, "y").astype(jnp.float32), 0) * 0.0625

    for axis in (("x", "core"), Z, "y"):
        stats = lax.psum(stats, axis)
    total_texts = txt_rows * 512
    image_grad = unnormalize(ux, rx, scale * image_accum)
    text_grad = unnormalize(uy, ry, scale * text_accum)
    loss = (stats[0] / total_texts).reshape(1)
    scale_grad = (scale * stats[1] / total_texts).reshape(1)
    bias_grad = (stats[2] / total_texts).reshape(1)
    return (image_grad, text_grad, loss, scale_grad, bias_grad)


def solution(mesh):
    fine = Mesh(mesh.devices.reshape(SIZES), AXES)
    split = P(AXES, None)
    return jax.shard_map(
        body,
        mesh=fine,
        in_specs=(split, split, P(), P(), P(), P()),
        out_specs=(split, split, P(), P(), P()),
        check_vma=False,
    )
```

```python
import jax
import jax.numpy as jnp
from jax import lax
from jax.experimental import pallas as pl
from jax.experimental.pallas import tpu as pltpu
from jax.sharding import Mesh, PartitionSpec as P

AXES = ("y", "zh", "zl", "x", "core")
SIZES = (8, 2, 4, 4, 2)
Z = ("zh", "zl")
UNIT = 16384.0


def normalize(rows):
    values = rows.astype(jnp.float32)
    radius = jnp.sqrt(jnp.sum(values * values, -1, keepdims=True) + 1e-06)
    unit = values / radius
    return (unit, radius, lax.reduce_precision(unit, 8, 7))


def unnormalize(unit, radius, grad):
    return (grad - unit * jnp.sum(unit * grad, -1, keepdims=True)) / radius


def swap(value, axis):
    return lax.all_to_all(value, axis, 0, 0, tiled=False)


def shifted(value, axis, steps):
    count = lax.axis_size(axis)
    return lax.ppermute(value, axis, [(i, (i + steps) % count) for i in range(count)])


def spread(block, axis):
    count = lax.axis_size(axis)
    return swap(jnp.broadcast_to(block[None], (count,) + block.shape), axis)


def forward_kernel(place, scalars, rows, cols, row_ids, col_ids, near, whole, stats, sums):
    step = pl.program_id(0)
    dots = lax.dot_general(
        rows[...], cols[...], (((1,), (1,)), ((), ())), preferred_element_type=jnp.float32
    )
    logits = scalars[0] * dots + scalars[1]
    match = row_ids[...] == col_ids[...]
    against = jnp.where(match, -logits, logits)
    decay = jnp.exp(-jnp.abs(against))
    objective = jnp.maximum(against, 0.0) + jnp.log1p(decay)
    weight = jnp.where(against >= 0.0, 1.0, decay) / (1.0 + decay)
    slope = jnp.where(match, -weight, weight)
    slopeb = slope.astype(jnp.bfloat16)
    near[...] = slopeb
    whole[...] = slopeb

    @pl.when(step == 0)
    def _():
        sums[...] = jnp.zeros_like(sums)

    for i, term in enumerate((objective, slope * dots, slope)):
        sums[i : i + 1, :] += jnp.sum(term, 0, keepdims=True)

    @pl.when(step == pl.num_programs(0) - 1)
    def _():
        stats[...] = jnp.broadcast_to(jnp.sum(sums[...], 1, keepdims=True), stats.shape)


def forward(x, scalars, rows, cols, row_ids, col_ids):
    parts = lax.axis_size("x")
    high, width = rows.shape[0] // parts, rows.shape[1]
    wide = cols.shape[0]
    part = lambda k, place: ((place[0] + k) % parts, 0)
    same = lambda k, place: (0, 0)
    slopes = jax.ShapeDtypeStruct((rows.shape[0], wide), jnp.bfloat16)
    return pl.pallas_call(
        forward_kernel,
        grid_spec=pltpu.PrefetchScalarGridSpec(
            num_scalar_prefetch=1,
            grid=(parts,),
            in_specs=[
                pl.BlockSpec(memory_space=pltpu.SMEM),
                pl.BlockSpec((high, width), part),
                pl.BlockSpec((wide, width), same),
                pl.BlockSpec((high, 1), part),
                pl.BlockSpec((1, wide), same),
            ],
            out_specs=[
                pl.BlockSpec((high, wide), lambda k, place: (k, 0)),
                pl.BlockSpec((high, wide), part),
                pl.BlockSpec((8, 128), same),
            ],
            scratch_shapes=[pltpu.VMEM((8, wide), jnp.float32)],
        ),
        out_shape=(slopes, slopes, jax.ShapeDtypeStruct((8, 128), jnp.float32)),
        compiler_params=pltpu.CompilerParams(vmem_limit_bytes=32 * 2**20),
        cost_estimate=pl.CostEstimate(flops=10**9, bytes_accessed=5 * 10**6, transcendentals=10**6),
        name="forward",
    )(x.reshape(1).astype(jnp.int32), scalars, rows, cols, row_ids, col_ids)


def body(images, texts, image_ids, text_ids, log_scale, bias):
    width = images.shape[1]
    img_rows = images.shape[0]
    txt_rows = texts.shape[0]
    y, x, core = (lax.axis_index(a) for a in ("y", "x", "core"))
    z = lax.axis_index(Z)
    scale = jnp.exp(log_scale[0])
    ux, rx, uxb = normalize(images)
    uy, ry, uyb = normalize(texts)

    own = spread(uxb.astype(jnp.bfloat16), "y").reshape(-1, width)
    cols = (uyb * UNIT).astype(jnp.float16)
    own, cols = lax.optimization_barrier((own, cols))
    rows = spread(own, "x").reshape(-1, width)
    cols = lax.all_gather(cols, Z + ("core",), axis=0, tiled=True)
    cols = (cols.astype(jnp.float32) * (1 / UNIT)).astype(jnp.bfloat16)
    cols = cols.reshape(8, 2, txt_rows, width)
    mine = lax.dynamic_index_in_dim(cols, core, 1, keepdims=False)
    theirs = lax.dynamic_index_in_dim(cols, 1 - core, 1, keepdims=False)
    cols = jnp.concatenate([mine, theirs], 0).reshape(-1, width)

    col_ids = text_ids.reshape(8, 8, 4, 2, txt_rows)
    col_ids = lax.dynamic_index_in_dim(col_ids, y, 0, keepdims=False)
    col_ids = lax.dynamic_index_in_dim(col_ids, x, 1, keepdims=False)
    mine = lax.dynamic_index_in_dim(col_ids, core, 1, keepdims=False)
    theirs = lax.dynamic_index_in_dim(col_ids, 1 - core, 1, keepdims=False)
    col_ids = jnp.concatenate([mine, theirs], 0).reshape(1, -1)
    row_ids = image_ids.reshape(8, 8, 4, 2, img_rows)
    row_ids = lax.dynamic_index_in_dim(row_ids, z, 1, keepdims=False)
    row_ids = lax.dynamic_index_in_dim(row_ids, core, 2, keepdims=False)
    row_ids = row_ids.transpose(1, 0, 2).reshape(-1, 1)

    near, whole, stats = forward(x, jnp.stack([scale, bias[0]]), rows, cols, row_ids, col_ids)
    stats = stats[:3, 0]

    half = cols.shape[0] // 2
    theirs = lax.dot_general(
        whole[:, half:], rows, (((0,), (0,)), ((), ())), preferred_element_type=jnp.float32
    )
    theirs = shifted(theirs, "core", 1)
    dcols = theirs + lax.dot_general(
        whole[:, :half], rows, (((0,), (0,)), ((), ())), preferred_element_type=jnp.float32
    )
    dcols = (dcols * 32.0).astype(jnp.float16).reshape(8, txt_rows, width)
    dcols = swap(dcols, Z)

    high = rows.shape[0] // 4
    back = {}
    for k in (1, 3, 2, 0):
        drows = 64.0 * jnp.dot(near[k * high : (k + 1) * high], cols, preferred_element_type=jnp.float32)
        back[k] = shifted(drows.astype(jnp.float16), "x", k) if k else drows
    drows = sum(part.astype(jnp.float32) for part in back.values())
    drows = (drows * 0.25).astype(jnp.float16).reshape(8, -1, width)
    drows = swap(drows, "y")

    for axis in (("x", "core"), Z, "y"):
        stats = lax.psum(stats, axis)
    total_texts = txt_rows * 512
    image_accum = jnp.sum(drows.astype(jnp.float32), 0) * 0.0625
    text_accum = jnp.sum(dcols.astype(jnp.float32), 0) * (1 / 32.0)
    image_grad = unnormalize(ux, rx, scale * image_accum)
    text_grad = unnormalize(uy, ry, scale * text_accum)
    loss = (stats[0] / total_texts).reshape(1)
    scale_grad = (scale * stats[1] / total_texts).reshape(1)
    bias_grad = (stats[2] / total_texts).reshape(1)
    return (image_grad, text_grad, loss, scale_grad, bias_grad)


def solution(mesh):
    fine = Mesh(mesh.devices.reshape(SIZES), AXES)
    split = P(AXES, None)
    return jax.shard_map(
        body,
        mesh=fine,
        in_specs=(split, split, P(), P(), P(), P()),
        out_specs=(split, split, P(), P(), P()),
        check_vma=False,
    )
```

```python
import jax
import jax.numpy as jnp
from jax import lax
from jax.experimental import pallas as pl
from jax.experimental.pallas import tpu as pltpu
from jax.sharding import Mesh, PartitionSpec as P

AXES = ("y", "zh", "zl", "x", "core")
SIZES = (8, 2, 4, 4, 2)
Z = ("zh", "zl")
UNIT = 16384.0


def normalize(rows):
    values = rows.astype(jnp.float32)
    radius = jnp.sqrt(jnp.sum(values * values, -1, keepdims=True) + 1e-06)
    unit = values / radius
    return (unit, radius, lax.reduce_precision(unit, 8, 7))


def unnormalize(unit, radius, grad):
    return (grad - unit * jnp.sum(unit * grad, -1, keepdims=True)) / radius


def swap(value, axis):
    return lax.all_to_all(value, axis, 0, 0, tiled=False)


def shifted(value, axis, steps):
    count = lax.axis_size(axis)
    return lax.ppermute(value, axis, [(i, (i + steps) % count) for i in range(count)])


def spread(block, axis):
    count = lax.axis_size(axis)
    return swap(jnp.broadcast_to(block[None], (count,) + block.shape), axis)


def pairs_kernel(place, scalars, rows, cols, row_ids, col_ids, slopes, theirs, mine):
    parts = 4
    high = rows.shape[0] // parts
    half = mine.shape[0]
    sums = [0.0, 0.0, 0.0]
    for k in range(parts):
        part = pl.ds(pl.multiple_of(lax.rem(place[0] + k, parts) * high, high), high)
        dots = lax.dot_general(
            rows[part, :], cols[...], (((1,), (1,)), ((), ())), preferred_element_type=jnp.float32
        )
        logits = scalars[0] * dots + scalars[1]
        match = row_ids[part, :] == col_ids[...]
        against = jnp.where(match, -logits, logits)
        decay = jnp.exp(-jnp.abs(against))
        objective = jnp.maximum(against, 0.0) + jnp.log1p(decay)
        weight = jnp.where(against >= 0.0, 1.0, decay) / (1.0 + decay)
        slope = jnp.where(match, -weight, weight)
        slopeb = slope.astype(jnp.bfloat16)
        slopes[k * high : (k + 1) * high, :] = slopeb
        for side, out in ((slopeb[:, :half], mine), (slopeb[:, half:], theirs)):
            product = lax.dot_general(
                side, rows[part, :], (((0,), (0,)), ((), ())), preferred_element_type=jnp.float32
            )
            out[:half, :] = product if k == 0 else out[:half, :] + product
        for i, term in enumerate((objective, slope * dots, slope)):
            sums[i] += jnp.sum(term, 0, keepdims=True)
    lane = lax.broadcasted_iota(jnp.int32, (8, theirs.shape[1]), 1)
    totals = jnp.zeros(lane.shape, jnp.float32)
    for i in range(3):
        totals = jnp.where(lane == i, jnp.sum(sums[i], 1, keepdims=True), totals)
    theirs[half:, :] = totals


def pairs(x, scalars, rows, cols, row_ids, col_ids):
    wide, width = cols.shape
    half = wide // 2
    vmem = pl.BlockSpec(memory_space=pltpu.VMEM)
    smem = pl.BlockSpec(memory_space=pltpu.SMEM)
    return pl.pallas_call(
        pairs_kernel,
        in_specs=[smem, smem, vmem, vmem, vmem, vmem],
        out_specs=[vmem, vmem, vmem],
        out_shape=(
            jax.ShapeDtypeStruct((rows.shape[0], wide), jnp.bfloat16),
            jax.ShapeDtypeStruct((half + 8, width), jnp.float32),
            jax.ShapeDtypeStruct((half, width), jnp.float32),
        ),
        compiler_params=pltpu.CompilerParams(vmem_limit_bytes=48 * 2**20),
        cost_estimate=pl.CostEstimate(flops=2 * 10**9, bytes_accessed=6 * 10**6, transcendentals=10**6),
        name="pairs",
    )(x.reshape(1).astype(jnp.int32), scalars, rows, cols, row_ids, col_ids)


def swap_sum(blocks, stats, axis):
    count, high, width = blocks.shape
    rider = jnp.concatenate(half_pieces(stats * (1 / 2048.0)) + [jnp.zeros((high - 3, 128), jnp.float16)], 0)
    rider = jnp.broadcast_to(rider[None], (count, high, 128))
    got = swap(jnp.concatenate([blocks, rider], 2), axis)
    stats = jnp.sum(got[:, :3, width:].astype(jnp.float32), (0, 1)).reshape(1, 128) * 2048.0
    return (jnp.sum(got[:, :, :width].astype(jnp.float32), 0), stats)


def half_pieces(value):
    pieces = []
    for _ in range(3):
        piece = lax.reduce_precision(value, 5, 10)
        pieces.append(piece.astype(jnp.float16))
        value = value - piece
    return pieces


def body(images, texts, image_ids, text_ids, log_scale, bias):
    width = images.shape[1]
    img_rows = images.shape[0]
    txt_rows = texts.shape[0]
    y, x, core = (lax.axis_index(a) for a in ("y", "x", "core"))
    z = lax.axis_index(Z)
    scale = jnp.exp(log_scale[0])
    ux, rx, uxb = normalize(images)
    uy, ry, uyb = normalize(texts)

    own = spread(uxb.astype(jnp.bfloat16), "y").reshape(-1, width)
    cols = (uyb * UNIT).astype(jnp.float16)
    own, cols = lax.optimization_barrier((own, cols))
    rows = spread(own, "x").reshape(-1, width)
    cols = lax.all_gather(cols, Z + ("core",), axis=0, tiled=True)
    cols = (cols.astype(jnp.float32) * (1 / UNIT)).astype(jnp.bfloat16)
    cols = cols.reshape(8, 2, txt_rows, width)
    mine = lax.dynamic_index_in_dim(cols, core, 1, keepdims=False)
    theirs = lax.dynamic_index_in_dim(cols, 1 - core, 1, keepdims=False)
    cols = jnp.concatenate([mine, theirs], 0).reshape(-1, width)

    col_ids = text_ids.reshape(8, 8, 4, 2, txt_rows)
    col_ids = lax.dynamic_index_in_dim(col_ids, y, 0, keepdims=False)
    col_ids = lax.dynamic_index_in_dim(col_ids, x, 1, keepdims=False)
    mine = lax.dynamic_index_in_dim(col_ids, core, 1, keepdims=False)
    theirs = lax.dynamic_index_in_dim(col_ids, 1 - core, 1, keepdims=False)
    col_ids = jnp.concatenate([mine, theirs], 0).reshape(1, -1)
    row_ids = image_ids.reshape(8, 8, 4, 2, img_rows)
    row_ids = lax.dynamic_index_in_dim(row_ids, z, 1, keepdims=False)
    row_ids = lax.dynamic_index_in_dim(row_ids, core, 2, keepdims=False)
    row_ids = row_ids.transpose(1, 0, 2).reshape(-1, 1)

    half = cols.shape[0] // 2
    high = rows.shape[0] // 4
    near, theirs, mine = pairs(x, jnp.stack([scale, bias[0]]), rows, cols, row_ids, col_ids)
    stats = theirs[half : half + 1, :128]

    dcols = shifted(theirs[:half], "core", 1) + mine
    stats = stats + shifted(stats, "core", 1)
    dcols, stats = swap_sum((dcols * 32.0).astype(jnp.float16).reshape(8, txt_rows, width), stats, Z)

    back = {}
    for k in (2, 1, 3, 0):
        drows = 64.0 * jnp.dot(near[k * high : (k + 1) * high], cols, preferred_element_type=jnp.float32)
        back[k] = shifted(drows.astype(jnp.float16), "x", k) if k else drows
    drows = sum(part.astype(jnp.float32) for part in back.values())
    drows = (drows * 0.25).astype(jnp.float16).reshape(8, -1, width)
    drows, stats = swap_sum(drows, stats, "y")
    for steps in (1, 2):
        stats = stats + shifted(stats, "x", steps)
    stats = stats[0]

    total_texts = txt_rows * 512
    image_accum = drows * 0.0625
    text_accum = dcols * (1 / 32.0)
    image_grad = unnormalize(ux, rx, scale * image_accum)
    text_grad = unnormalize(uy, ry, scale * text_accum)
    loss = (stats[0] / total_texts).reshape(1)
    scale_grad = (scale * stats[1] / total_texts).reshape(1)
    bias_grad = (stats[2] / total_texts).reshape(1)
    return (image_grad, text_grad, loss, scale_grad, bias_grad)


def solution(mesh):
    fine = Mesh(mesh.devices.reshape(SIZES), AXES)
    split = P(AXES, None)
    return jax.shard_map(
        body,
        mesh=fine,
        in_specs=(split, split, P(), P(), P(), P()),
        out_specs=(split, split, P(), P(), P()),
        check_vma=False,
    )
```

```python
import jax
import jax.numpy as jnp
from jax import lax
from jax.experimental import pallas as pl
from jax.experimental.pallas import tpu as pltpu
from jax.sharding import Mesh, PartitionSpec as P

AXES = ("y", "zh", "zl", "x", "core")
SIZES = (8, 2, 4, 4, 2)
Z = ("zh", "zl")
UNIT = 16384.0


def normalize(rows):
    values = rows.astype(jnp.float32)
    radius = jnp.sqrt(jnp.sum(values * values, -1, keepdims=True) + 1e-06)
    unit = values / radius
    return (unit, radius, lax.reduce_precision(unit, 8, 7))


def unnormalize(unit, radius, grad):
    return (grad - unit * jnp.sum(unit * grad, -1, keepdims=True)) / radius


def swap(value, axis):
    return lax.all_to_all(value, axis, 0, 0, tiled=False)


def shifted(value, axis, steps):
    count = lax.axis_size(axis)
    return lax.ppermute(value, axis, [(i, (i + steps) % count) for i in range(count)])


def spread(block, axis):
    count = lax.axis_size(axis)
    return swap(jnp.broadcast_to(block[None], (count,) + block.shape), axis)


def slopes_kernel(place, scalars, rows, cols, row_ids, col_ids, slopes, totals):
    parts = 4
    high = rows.shape[0] // parts
    sums = [0.0, 0.0, 0.0]
    for k in range(parts):
        part = pl.ds(pl.multiple_of(lax.rem(place[0] + k, parts) * high, high), high)
        dots = lax.dot_general(
            rows[part, :], cols[...], (((1,), (1,)), ((), ())), preferred_element_type=jnp.float32
        )
        logits = scalars[0] * dots + scalars[1]
        match = row_ids[part, :] == col_ids[...]
        against = jnp.where(match, -logits, logits)
        decay = jnp.exp(-jnp.abs(against))
        objective = jnp.maximum(against, 0.0) + jnp.log1p(decay)
        weight = jnp.where(against >= 0.0, 1.0, decay) / (1.0 + decay)
        slope = jnp.where(match, -weight, weight)
        slopes[k * high : (k + 1) * high, :] = slope.astype(jnp.bfloat16)
        for i, term in enumerate((objective, slope * dots, slope)):
            sums[i] += jnp.sum(term, 0, keepdims=True)
    lane = lax.broadcasted_iota(jnp.int32, totals.shape, 1)
    total = jnp.zeros(totals.shape, jnp.float32)
    for i in range(3):
        total = jnp.where(lane == i, jnp.sum(sums[i], 1, keepdims=True), total)
    totals[...] = total


def text_kernel(place, rows, slopes, totals, theirs, mine):
    parts = 4
    high = rows.shape[0] // parts
    half = mine.shape[0]
    for side, out in ((slice(half, None), theirs), (slice(0, half), mine)):
        for k in range(parts):
            part = pl.ds(pl.multiple_of(lax.rem(place[0] + k, parts) * high, high), high)
            product = lax.dot_general(
                slopes[k * high : (k + 1) * high, side],
                rows[part, :],
                (((0,), (0,)), ((), ())),
                preferred_element_type=jnp.float32,
            )
            out[:half, :] = product if k == 0 else out[:half, :] + product
    theirs[half:, :] = totals[...]


VMEM = pl.BlockSpec(memory_space=pltpu.VMEM)
SMEM = pl.BlockSpec(memory_space=pltpu.SMEM)


def slopes_of(place, scalars, rows, cols, row_ids, col_ids):
    wide, width = cols.shape
    return pl.pallas_call(
        slopes_kernel,
        in_specs=[SMEM, SMEM, VMEM, VMEM, VMEM, VMEM],
        out_specs=[VMEM, VMEM],
        out_shape=(
            jax.ShapeDtypeStruct((rows.shape[0], wide), jnp.bfloat16),
            jax.ShapeDtypeStruct((8, width), jnp.float32),
        ),
        compiler_params=pltpu.CompilerParams(vmem_limit_bytes=48 * 2**20),
        cost_estimate=pl.CostEstimate(flops=10**9, bytes_accessed=4 * 10**6, transcendentals=10**6),
        name="slopes",
    )(place, scalars, rows, cols, row_ids, col_ids)


def text_products(place, rows, slopes, totals):
    half, width = slopes.shape[1] // 2, rows.shape[1]
    return pl.pallas_call(
        text_kernel,
        in_specs=[SMEM, VMEM, VMEM, VMEM],
        out_specs=[VMEM, VMEM],
        out_shape=(
            jax.ShapeDtypeStruct((half + 8, width), jnp.float32),
            jax.ShapeDtypeStruct((half, width), jnp.float32),
        ),
        compiler_params=pltpu.CompilerParams(vmem_limit_bytes=48 * 2**20),
        cost_estimate=pl.CostEstimate(flops=10**9, bytes_accessed=5 * 10**6, transcendentals=0),
        name="text_products",
    )(place, rows, slopes, totals)


def swap_sum(blocks, stats, axis):
    count, high, width = blocks.shape
    rider = jnp.concatenate(half_pieces(stats * (1 / 2048.0)) + [jnp.zeros((high - 3, 128), jnp.float16)], 0)
    rider = jnp.broadcast_to(rider[None], (count, high, 128))
    got = swap(jnp.concatenate([blocks, rider], 2), axis)
    stats = jnp.sum(got[:, :3, width:].astype(jnp.float32), (0, 1)).reshape(1, 128) * 2048.0
    return (jnp.sum(got[:, :, :width].astype(jnp.float32), 0), stats)


def half_pieces(value):
    pieces = []
    for _ in range(3):
        piece = lax.reduce_precision(value, 5, 10)
        pieces.append(piece.astype(jnp.float16))
        value = value - piece
    return pieces


def body(images, texts, image_ids, text_ids, log_scale, bias):
    width = images.shape[1]
    img_rows = images.shape[0]
    txt_rows = texts.shape[0]
    y, x, core = (lax.axis_index(a) for a in ("y", "x", "core"))
    z = lax.axis_index(Z)
    scale = jnp.exp(log_scale[0])
    ux, rx, uxb = normalize(images)
    uy, ry, uyb = normalize(texts)

    own = spread(uxb.astype(jnp.bfloat16), "y").reshape(-1, width)
    cols = (uyb * UNIT).astype(jnp.float16)
    first = lax.all_gather(cols[:, :640], Z + ("core",), axis=0, tiled=True)
    own, second, first = lax.optimization_barrier((own, cols[:, 640:], first))
    rows = spread(own, "x").reshape(-1, width)
    second = lax.all_gather(second, Z + ("core",), axis=0, tiled=True)
    cols = jnp.concatenate([first, second], 1)
    cols = (cols.astype(jnp.float32) * (1 / UNIT)).astype(jnp.bfloat16)
    cols = cols.reshape(8, 2, txt_rows, width)
    mine = lax.dynamic_index_in_dim(cols, core, 1, keepdims=False)
    theirs = lax.dynamic_index_in_dim(cols, 1 - core, 1, keepdims=False)
    cols = jnp.concatenate([mine, theirs], 0).reshape(-1, width)

    col_ids = text_ids.reshape(8, 8, 4, 2, txt_rows)
    col_ids = lax.dynamic_index_in_dim(col_ids, y, 0, keepdims=False)
    col_ids = lax.dynamic_index_in_dim(col_ids, x, 1, keepdims=False)
    mine = lax.dynamic_index_in_dim(col_ids, core, 1, keepdims=False)
    theirs = lax.dynamic_index_in_dim(col_ids, 1 - core, 1, keepdims=False)
    col_ids = jnp.concatenate([mine, theirs], 0).reshape(1, -1)
    row_ids = image_ids.reshape(8, 8, 4, 2, img_rows)
    row_ids = lax.dynamic_index_in_dim(row_ids, z, 1, keepdims=False)
    row_ids = lax.dynamic_index_in_dim(row_ids, core, 2, keepdims=False)
    row_ids = row_ids.transpose(1, 0, 2).reshape(-1, 1)

    half = cols.shape[0] // 2
    high = rows.shape[0] // 4
    place = x.reshape(1).astype(jnp.int32)
    near, totals = slopes_of(place, jnp.stack([scale, bias[0]]), rows, cols, row_ids, col_ids)

    back = {}
    for k in (2, 1, 3, 0):
        drows = 64.0 * jnp.dot(near[k * high : (k + 1) * high], cols, preferred_element_type=jnp.float32)
        back[k] = drows.astype(jnp.float16) if k else drows
    near, back[1], back[2], back[3] = lax.optimization_barrier((near, back[1], back[2], back[3]))
    for k in (1, 3, 2):
        back[k] = shifted(back[k], "x", k)

    theirs, mine = text_products(place, rows, near, totals)
    got = shifted(theirs, "core", 1)
    dcols = ((got[:half] + mine) * 32.0).astype(jnp.float16).reshape(8, txt_rows, width)
    dcols, back[1], back[3] = lax.optimization_barrier((dcols, back[1], back[3]))
    dcols, stats = swap_sum(dcols, got[half : half + 1, :128] + totals[:1, :128], Z)
    for steps in (1, 2):
        stats = stats + shifted(stats, "x", steps)

    drows = sum(part.astype(jnp.float32) for part in back.values())
    drows = (drows * 0.25).astype(jnp.float16).reshape(8, -1, width)
    drows, stats = swap_sum(drows, stats, "y")
    stats = stats[0]

    total_texts = txt_rows * 512
    image_accum = drows * 0.0625
    text_accum = dcols * (1 / 32.0)
    image_grad = unnormalize(ux, rx, scale * image_accum)
    text_grad = unnormalize(uy, ry, scale * text_accum)
    lane = lax.iota(jnp.int32, stats.shape[0])
    stats = stats * jnp.where(lane == 1, scale, 1.0) * (1.0 / total_texts)
    loss, scale_grad, bias_grad = stats[0:1], stats[1:2], stats[2:3]
    return (image_grad, text_grad, loss, scale_grad, bias_grad)


def solution(mesh):
    fine = Mesh(mesh.devices.reshape(SIZES), AXES)
    split = P(AXES, None)
    return jax.shard_map(
        body,
        mesh=fine,
        in_specs=(split, split, P(), P(), P(), P()),
        out_specs=(split, split, P(), P(), P()),
        check_vma=False,
    )
```

```python
import jax
import jax.numpy as jnp
from jax import lax
from jax.experimental import pallas as pl
from jax.experimental.pallas import tpu as pltpu
from jax.sharding import Mesh, PartitionSpec as P

AXES = ("y", "zh", "zl", "x", "core")
SIZES = (8, 2, 4, 4, 2)
Z = ("zh", "zl")
UNIT = 16384.0


def normalize(rows):
    values = rows.astype(jnp.float32)
    radius = jnp.sqrt(jnp.sum(values * values, -1, keepdims=True) + 1e-06)
    unit = values / radius
    return (unit, radius, lax.reduce_precision(unit, 8, 7))


def unnormalize(unit, radius, grad):
    return (grad - unit * jnp.sum(unit * grad, -1, keepdims=True)) / radius


def swap(value, axis):
    return lax.all_to_all(value, axis, 0, 0, tiled=False)


def shifted(value, axis, steps):
    count = lax.axis_size(axis)
    return lax.ppermute(value, axis, [(i, (i + steps) % count) for i in range(count)])


def spread(block, axis):
    count = lax.axis_size(axis)
    return swap(jnp.broadcast_to(block[None], (count,) + block.shape), axis)


def slopes_kernel(place, scalars, rows, cols, row_ids, col_ids, slopes, totals):
    parts = 4
    high = rows.shape[0] // parts
    sums = [0.0, 0.0, 0.0]
    for k in range(parts):
        part = pl.ds(pl.multiple_of(lax.rem(place[0] + k, parts) * high, high), high)
        dots = lax.dot_general(
            rows[part, :], cols[...], (((1,), (1,)), ((), ())), preferred_element_type=jnp.float32
        )
        logits = scalars[0] * dots + scalars[1]
        match = row_ids[part, :] == col_ids[...]
        against = jnp.where(match, -logits, logits)
        decay = jnp.exp(-jnp.abs(against))
        objective = jnp.maximum(against, 0.0) + jnp.log1p(decay)
        weight = jnp.where(against >= 0.0, 1.0, decay) / (1.0 + decay)
        slope = jnp.where(match, -weight, weight)
        slopes[k * high : (k + 1) * high, :] = slope.astype(jnp.bfloat16)
        for i, term in enumerate((objective, slope * dots, slope)):
            sums[i] += jnp.sum(term, 0, keepdims=True)
    lane = lax.broadcasted_iota(jnp.int32, totals.shape, 1)
    total = jnp.zeros(totals.shape, jnp.float32)
    for i in range(3):
        total = jnp.where(lane == i, jnp.sum(sums[i], 1, keepdims=True), total)
    totals[...] = total


def text_kernel(place, rows, slopes, totals, theirs, mine):
    parts = 4
    high = rows.shape[0] // parts
    half = mine.shape[0]
    for side, out in ((slice(half, None), theirs), (slice(0, half), mine)):
        for k in range(parts):
            part = pl.ds(pl.multiple_of(lax.rem(place[0] + k, parts) * high, high), high)
            product = lax.dot_general(
                slopes[k * high : (k + 1) * high, side],
                rows[part, :],
                (((0,), (0,)), ((), ())),
                preferred_element_type=jnp.float32,
            )
            out[:half, :] = product if k == 0 else out[:half, :] + product
    theirs[half:, :] = totals[...]


VMEM = pl.BlockSpec(memory_space=pltpu.VMEM)
SMEM = pl.BlockSpec(memory_space=pltpu.SMEM)


def slopes_of(place, scalars, rows, cols, row_ids, col_ids):
    wide, width = cols.shape
    return pl.pallas_call(
        slopes_kernel,
        in_specs=[SMEM, SMEM, VMEM, VMEM, VMEM, VMEM],
        out_specs=[VMEM, VMEM],
        out_shape=(
            jax.ShapeDtypeStruct((rows.shape[0], wide), jnp.bfloat16),
            jax.ShapeDtypeStruct((8, width), jnp.float32),
        ),
        compiler_params=pltpu.CompilerParams(vmem_limit_bytes=48 * 2**20),
        cost_estimate=pl.CostEstimate(flops=10**9, bytes_accessed=4 * 10**6, transcendentals=10**6),
        name="slopes",
    )(place, scalars, rows, cols, row_ids, col_ids)


def text_products(place, rows, slopes, totals):
    half, width = slopes.shape[1] // 2, rows.shape[1]
    return pl.pallas_call(
        text_kernel,
        in_specs=[SMEM, VMEM, VMEM, VMEM],
        out_specs=[VMEM, VMEM],
        out_shape=(
            jax.ShapeDtypeStruct((half + 8, width), jnp.float32),
            jax.ShapeDtypeStruct((half, width), jnp.float32),
        ),
        compiler_params=pltpu.CompilerParams(vmem_limit_bytes=48 * 2**20),
        cost_estimate=pl.CostEstimate(flops=10**9, bytes_accessed=5 * 10**6, transcendentals=0),
        name="text_products",
    )(place, rows, slopes, totals)


def swap_sum(blocks, stats, axis):
    count, high, width = blocks.shape
    rider = jnp.concatenate(half_pieces(stats * (1 / 2048.0)) + [jnp.zeros((high - 3, 128), jnp.float16)], 0)
    rider = jnp.broadcast_to(rider[None], (count, high, 128))
    got = swap(jnp.concatenate([blocks, rider], 2), axis)
    stats = jnp.sum(got[:, :3, width:].astype(jnp.float32), (0, 1)).reshape(1, 128) * 2048.0
    return (jnp.sum(got[:, :, :width].astype(jnp.float32), 0), stats)


def half_pieces(value):
    pieces = []
    for _ in range(3):
        piece = lax.reduce_precision(value, 5, 10)
        pieces.append(piece.astype(jnp.float16))
        value = value - piece
    return pieces


def body(images, texts, image_ids, text_ids, log_scale, bias):
    width = images.shape[1]
    img_rows = images.shape[0]
    txt_rows = texts.shape[0]
    y, x, core = (lax.axis_index(a) for a in ("y", "x", "core"))
    z = lax.axis_index(Z)
    scale = jnp.exp(log_scale[0])
    ux, rx, uxb = normalize(images)
    uy, ry, uyb = normalize(texts)

    own = spread(uxb.astype(jnp.bfloat16), "y").reshape(-1, width)
    cols = (uyb * UNIT).astype(jnp.float16)
    own, cols = lax.optimization_barrier((own, cols))
    rows = spread(own, "x").reshape(-1, width)
    cols = lax.all_gather(cols, Z + ("core",), axis=0, tiled=True)
    cols = (cols.astype(jnp.float32) * (1 / UNIT)).astype(jnp.bfloat16)
    cols = cols.reshape(8, 2, txt_rows, width)
    mine = lax.dynamic_index_in_dim(cols, core, 1, keepdims=False)
    theirs = lax.dynamic_index_in_dim(cols, 1 - core, 1, keepdims=False)
    cols = jnp.concatenate([mine, theirs], 0).reshape(-1, width)

    col_ids = text_ids.reshape(8, 8, 4, 2, txt_rows)
    col_ids = lax.dynamic_index_in_dim(col_ids, y, 0, keepdims=False)
    col_ids = lax.dynamic_index_in_dim(col_ids, x, 1, keepdims=False)
    mine = lax.dynamic_index_in_dim(col_ids, core, 1, keepdims=False)
    theirs = lax.dynamic_index_in_dim(col_ids, 1 - core, 1, keepdims=False)
    col_ids = jnp.concatenate([mine, theirs], 0).reshape(1, -1)
    row_ids = image_ids.reshape(8, 8, 4, 2, img_rows)
    row_ids = lax.dynamic_index_in_dim(row_ids, z, 1, keepdims=False)
    row_ids = lax.dynamic_index_in_dim(row_ids, core, 2, keepdims=False)
    row_ids = row_ids.transpose(1, 0, 2).reshape(-1, 1)

    half = cols.shape[0] // 2
    high = rows.shape[0] // 4
    place = x.reshape(1).astype(jnp.int32)
    near, totals = slopes_of(place, jnp.stack([scale, bias[0]]), rows, cols, row_ids, col_ids)

    back = {}
    for k in (2, 1, 3, 0):
        drows = 64.0 * jnp.dot(near[k * high : (k + 1) * high], cols, preferred_element_type=jnp.float32)
        back[k] = drows.astype(jnp.float16) if k else drows
    for k in (2, 1, 3):
        back[k] = shifted(back[k], "x", k)

    theirs, mine = text_products(place, rows, near, totals)
    got = shifted(theirs, "core", 1)
    dcols = ((got[:half] + mine) * 32.0).astype(jnp.float16).reshape(8, txt_rows, width)
    dcols, stats = swap_sum(dcols, got[half : half + 1, :128] + totals[:1, :128], Z)
    for steps in (1, 2):
        stats = stats + shifted(stats, "x", steps)

    drows = sum(part.astype(jnp.float32) for part in back.values())
    drows = (drows * 0.25).astype(jnp.float16).reshape(8, -1, width)
    drows, stats = swap_sum(drows, stats, "y")
    stats = stats[0]

    total_texts = txt_rows * 512
    image_accum = drows * 0.0625
    text_accum = dcols * (1 / 32.0)
    image_grad = unnormalize(ux, rx, scale * image_accum)
    text_grad = unnormalize(uy, ry, scale * text_accum)
    lane = lax.iota(jnp.int32, stats.shape[0])
    stats = stats * jnp.where(lane == 1, scale, 1.0) * (1.0 / total_texts)
    loss, scale_grad, bias_grad = stats[0:1], stats[1:2], stats[2:3]
    return (image_grad, text_grad, loss, scale_grad, bias_grad)


def solution(mesh):
    fine = Mesh(mesh.devices.reshape(SIZES), AXES)
    split = P(AXES, None)
    return jax.shard_map(
        body,
        mesh=fine,
        in_specs=(split, split, P(), P(), P(), P()),
        out_specs=(split, split, P(), P(), P()),
        check_vma=False,
    )
```

```python
import jax
import jax.numpy as jnp
from jax import lax
from jax.experimental import pallas as pl
from jax.experimental.pallas import tpu as pltpu
from jax.sharding import Mesh, PartitionSpec as P

AXES = ("y", "zh", "zl", "x", "core")
SIZES = (8, 2, 4, 4, 2)
Z = ("zh", "zl")
UNIT = 16384.0


def normalize(rows):
    values = rows.astype(jnp.float32)
    radius = jnp.sqrt(jnp.sum(values * values, -1, keepdims=True) + 1e-06)
    unit = values / radius
    return (unit, radius, lax.reduce_precision(unit, 8, 7))


def unnormalize(unit, radius, grad):
    return (grad - unit * jnp.sum(unit * grad, -1, keepdims=True)) / radius


def swap(value, axis):
    return lax.all_to_all(value, axis, 0, 0, tiled=False)


def shifted(value, axis, steps):
    count = lax.axis_size(axis)
    return lax.ppermute(value, axis, [(i, (i + steps) % count) for i in range(count)])


def spread(block, axis):
    count = lax.axis_size(axis)
    return swap(jnp.broadcast_to(block[None], (count,) + block.shape), axis)


def slopes_kernel(place, scalars, rows, cols, row_ids, col_ids, slopes, totals):
    parts = 4
    high = rows.shape[0] // parts
    sums = [0.0, 0.0, 0.0]
    for k in range(parts):
        part = pl.ds(pl.multiple_of(lax.rem(place[0] + k, parts) * high, high), high)
        dots = lax.dot_general(
            rows[part, :], cols[...], (((1,), (1,)), ((), ())), preferred_element_type=jnp.float32
        )
        logits = scalars[0] * dots + scalars[1]
        match = row_ids[part, :] == col_ids[...]
        against = jnp.where(match, -logits, logits)
        decay = jnp.exp(-jnp.abs(against))
        objective = jnp.maximum(against, 0.0) + jnp.log1p(decay)
        weight = jnp.where(against >= 0.0, 1.0, decay) / (1.0 + decay)
        slope = jnp.where(match, -weight, weight)
        slopes[k * high : (k + 1) * high, :] = slope.astype(jnp.bfloat16)
        for i, term in enumerate((objective, slope * dots, slope)):
            sums[i] += jnp.sum(term, 0, keepdims=True)
    lane = lax.broadcasted_iota(jnp.int32, totals.shape, 1)
    total = jnp.zeros(totals.shape, jnp.float32)
    for i in range(3):
        total = jnp.where(lane == i, jnp.sum(sums[i], 1, keepdims=True), total)
    totals[...] = total


def text_kernel(place, rows, slopes, totals, theirs, mine):
    parts = 4
    high = rows.shape[0] // parts
    half = mine.shape[0]
    for side, out in ((slice(half, None), theirs), (slice(0, half), mine)):
        for k in range(parts):
            part = pl.ds(pl.multiple_of(lax.rem(place[0] + k, parts) * high, high), high)
            product = lax.dot_general(
                slopes[k * high : (k + 1) * high, side],
                rows[part, :],
                (((0,), (0,)), ((), ())),
                preferred_element_type=jnp.float32,
            )
            out[:half, :] = product if k == 0 else out[:half, :] + product
    theirs[half:, :] = totals[...]


VMEM = pl.BlockSpec(memory_space=pltpu.VMEM)
SMEM = pl.BlockSpec(memory_space=pltpu.SMEM)


def slopes_of(place, scalars, rows, cols, row_ids, col_ids):
    wide, width = cols.shape
    return pl.pallas_call(
        slopes_kernel,
        in_specs=[SMEM, SMEM, VMEM, VMEM, VMEM, VMEM],
        out_specs=[VMEM, VMEM],
        out_shape=(
            jax.ShapeDtypeStruct((rows.shape[0], wide), jnp.bfloat16),
            jax.ShapeDtypeStruct((8, width), jnp.float32),
        ),
        compiler_params=pltpu.CompilerParams(vmem_limit_bytes=48 * 2**20),
        cost_estimate=pl.CostEstimate(flops=10**9, bytes_accessed=4 * 10**6, transcendentals=10**6),
        name="slopes",
    )(place, scalars, rows, cols, row_ids, col_ids)


def text_products(place, rows, slopes, totals):
    half, width = slopes.shape[1] // 2, rows.shape[1]
    return pl.pallas_call(
        text_kernel,
        in_specs=[SMEM, VMEM, VMEM, VMEM],
        out_specs=[VMEM, VMEM],
        out_shape=(
            jax.ShapeDtypeStruct((half + 8, width), jnp.float32),
            jax.ShapeDtypeStruct((half, width), jnp.float32),
        ),
        compiler_params=pltpu.CompilerParams(vmem_limit_bytes=48 * 2**20),
        cost_estimate=pl.CostEstimate(flops=10**9, bytes_accessed=5 * 10**6, transcendentals=0),
        name="text_products",
    )(place, rows, slopes, totals)


def swap_sum(blocks, stats, axis):
    count, high, width = blocks.shape
    rider = jnp.concatenate(half_pieces(stats * (1 / 2048.0)) + [jnp.zeros((high - 3, 128), jnp.float16)], 0)
    rider = jnp.broadcast_to(rider[None], (count, high, 128))
    got = swap(jnp.concatenate([blocks, rider], 2), axis)
    stats = jnp.sum(got[:, :3, width:].astype(jnp.float32), (0, 1)).reshape(1, 128) * 2048.0
    return (jnp.sum(got[:, :, :width].astype(jnp.float32), 0), stats)


def half_pieces(value):
    pieces = []
    for _ in range(3):
        piece = lax.reduce_precision(value, 5, 10)
        pieces.append(piece.astype(jnp.float16))
        value = value - piece
    return pieces


def body(images, texts, image_ids, text_ids, log_scale, bias):
    width = images.shape[1]
    img_rows = images.shape[0]
    txt_rows = texts.shape[0]
    y, x, core = (lax.axis_index(a) for a in ("y", "x", "core"))
    z = lax.axis_index(Z)
    scale = jnp.exp(log_scale[0])
    ux, rx, uxb = normalize(images)
    uy, ry, uyb = normalize(texts)

    own = spread((uxb * UNIT).astype(jnp.float16), "y").reshape(-1, width)
    cols = lax.all_gather((uyb * UNIT).astype(jnp.float16), Z + ("core",), axis=0, tiled=True)
    own, cols = lax.optimization_barrier((own, cols))
    rows = lax.all_gather(own, "x", axis=0, tiled=True)
    rows = (rows.astype(jnp.float32) * (1 / UNIT)).astype(jnp.bfloat16)
    cols = (cols.astype(jnp.float32) * (1 / UNIT)).astype(jnp.bfloat16)
    cols = cols.reshape(8, 2, txt_rows, width)
    mine = lax.dynamic_index_in_dim(cols, core, 1, keepdims=False)
    theirs = lax.dynamic_index_in_dim(cols, 1 - core, 1, keepdims=False)
    cols = jnp.concatenate([mine, theirs], 0).reshape(-1, width)

    col_ids = text_ids.reshape(8, 8, 4, 2, txt_rows)
    col_ids = lax.dynamic_index_in_dim(col_ids, y, 0, keepdims=False)
    col_ids = lax.dynamic_index_in_dim(col_ids, x, 1, keepdims=False)
    mine = lax.dynamic_index_in_dim(col_ids, core, 1, keepdims=False)
    theirs = lax.dynamic_index_in_dim(col_ids, 1 - core, 1, keepdims=False)
    col_ids = jnp.concatenate([mine, theirs], 0).reshape(1, -1)
    row_ids = image_ids.reshape(8, 8, 4, 2, img_rows)
    row_ids = lax.dynamic_index_in_dim(row_ids, z, 1, keepdims=False)
    row_ids = lax.dynamic_index_in_dim(row_ids, core, 2, keepdims=False)
    row_ids = row_ids.transpose(1, 0, 2).reshape(-1, 1)

    half = cols.shape[0] // 2
    high = rows.shape[0] // 4
    place = x.reshape(1).astype(jnp.int32)
    near, totals = slopes_of(place, jnp.stack([scale, bias[0]]), rows, cols, row_ids, col_ids)

    back = {}
    for k in (2, 1, 3, 0):
        drows = 64.0 * jnp.dot(near[k * high : (k + 1) * high], cols, preferred_element_type=jnp.float32)
        back[k] = drows.astype(jnp.float16) if k else drows
    for k in (2, 1, 3):
        back[k] = shifted(back[k], "x", k)

    theirs, mine = text_products(place, rows, near, totals)
    got = shifted(theirs, "core", 1)
    dcols = ((got[:half] + mine) * 32.0).astype(jnp.float16).reshape(8, txt_rows, width)
    dcols, stats = swap_sum(dcols, got[half : half + 1, :128] + totals[:1, :128], Z)
    stats = jnp.sum(spread(stats, "x"), 0)

    drows = sum(part.astype(jnp.float32) for part in back.values())
    drows = (drows * 0.25).astype(jnp.float16).reshape(8, -1, width)
    drows, stats = swap_sum(drows, stats, "y")
    stats = stats[0]

    total_texts = txt_rows * 512
    image_accum = drows * 0.0625
    text_accum = dcols * (1 / 32.0)
    image_grad = unnormalize(ux, rx, scale * image_accum)
    text_grad = unnormalize(uy, ry, scale * text_accum)
    lane = lax.iota(jnp.int32, stats.shape[0])
    stats = stats * jnp.where(lane == 1, scale, 1.0) * (1.0 / total_texts)
    loss, scale_grad, bias_grad = stats[0:1], stats[1:2], stats[2:3]
    return (image_grad, text_grad, loss, scale_grad, bias_grad)


def solution(mesh):
    fine = Mesh(mesh.devices.reshape(SIZES), AXES)
    split = P(AXES, None)
    return jax.shard_map(
        body,
        mesh=fine,
        in_specs=(split, split, P(), P(), P(), P()),
        out_specs=(split, split, P(), P(), P()),
        check_vma=False,
    )
```

```python
import functools

import jax
import jax.numpy as jnp
from jax import lax
from jax.experimental import pallas as pl
from jax.experimental.pallas import tpu as pltpu
from jax.sharding import Mesh, PartitionSpec as P

AXES = ("y", "zh", "zl", "x", "core")
SIZES = (8, 2, 4, 4, 2)
Z = ("zh", "zl")
UNIT = 16384.0


VMEM = pl.BlockSpec(memory_space=pltpu.VMEM)
SMEM = pl.BlockSpec(memory_space=pltpu.SMEM)


def normalize_kernel(images, texts, spread_images, text_bits, ux, rx, uy, ry):
    for rows, unit, radius in ((images, ux, rx), (texts, uy, ry)):
        values = rows[...].astype(jnp.float32)
        length = jnp.sqrt(jnp.sum(values * values, -1, keepdims=True) + 1e-06)
        unit[...] = values / length
        radius[...] = jnp.broadcast_to(length, radius.shape)
    for i in range(spread_images.shape[0]):
        spread_images[i] = ux[...].astype(jnp.bfloat16)
    text_bits[...] = uy[...].astype(jnp.bfloat16)


def normalize(images, texts, copies):
    shape = jax.ShapeDtypeStruct
    full = lambda rows: [shape(rows.shape, jnp.float32), shape((rows.shape[0], 128), jnp.float32)]
    return pl.pallas_call(
        normalize_kernel,
        in_specs=[VMEM] * 2,
        out_specs=[VMEM] * 6,
        out_shape=[shape((copies,) + images.shape, jnp.bfloat16), shape(texts.shape, jnp.bfloat16)]
        + full(images)
        + full(texts),
        compiler_params=pltpu.CompilerParams(vmem_limit_bytes=8 * 2**20),
        cost_estimate=pl.CostEstimate(flops=10**6, bytes_accessed=10**6, transcendentals=1000),
        name="normalize",
    )(images, texts)


def unnormalize(unit, radius, grad):
    return (grad - unit * jnp.sum(unit * grad, -1, keepdims=True)) / radius


def swap(value, axis):
    return lax.all_to_all(value, axis, 0, 0, tiled=False)


def shifted(value, axis, steps):
    count = lax.axis_size(axis)
    return lax.ppermute(value, axis, [(i, (i + steps) % count) for i in range(count)])


def spread(block, axis):
    count = lax.axis_size(axis)
    return swap(jnp.broadcast_to(block[None], (count,) + block.shape), axis)


def slopes_kernel(place, scalars, rows, cols, row_ids, col_ids, slopes, totals):
    parts = 4
    high = rows.shape[0] // parts
    sums = [0.0, 0.0, 0.0]
    for k in range(parts):
        part = pl.ds(pl.multiple_of(lax.rem(place[0] + k, parts) * high, high), high)
        dots = lax.dot_general(
            rows[part, :], cols[...], (((1,), (1,)), ((), ())), preferred_element_type=jnp.float32
        )
        logits = scalars[0] * dots + scalars[1]
        match = row_ids[part, :] == col_ids[...]
        against = jnp.where(match, -logits, logits)
        decay = jnp.exp(-jnp.abs(against))
        objective = jnp.maximum(against, 0.0) + jnp.log1p(decay)
        weight = jnp.where(against >= 0.0, 1.0, decay) / (1.0 + decay)
        slope = jnp.where(match, -weight, weight)
        slopes[k * high : (k + 1) * high, :] = slope.astype(jnp.bfloat16)
        for i, term in enumerate((objective, slope * dots, slope)):
            sums[i] += jnp.sum(term, 0, keepdims=True)
    lane = lax.broadcasted_iota(jnp.int32, totals.shape, 1)
    total = jnp.zeros(totals.shape, jnp.float32)
    for i in range(3):
        total = jnp.where(lane == i, jnp.sum(sums[i], 1, keepdims=True), total)
    totals[...] = total


def text_kernel(side, place, rows, slopes, totals, out):
    parts = 4
    high = rows.shape[0] // parts
    half = slopes.shape[1] // 2
    for k in range(parts):
        part = pl.ds(pl.multiple_of(lax.rem(place[0] + k, parts) * high, high), high)
        product = lax.dot_general(
            slopes[k * high : (k + 1) * high, side * half : (side + 1) * half],
            rows[part, :],
            (((0,), (0,)), ((), ())),
            preferred_element_type=jnp.float32,
        )
        out[:half, :] = product if k == 0 else out[:half, :] + product
    if side:
        out[half:, :] = totals[...]


def slopes_of(place, scalars, rows, cols, row_ids, col_ids):
    wide, width = cols.shape
    return pl.pallas_call(
        slopes_kernel,
        in_specs=[SMEM, SMEM, VMEM, VMEM, VMEM, VMEM],
        out_specs=[VMEM, VMEM],
        out_shape=(
            jax.ShapeDtypeStruct((rows.shape[0], wide), jnp.bfloat16),
            jax.ShapeDtypeStruct((8, width), jnp.float32),
        ),
        compiler_params=pltpu.CompilerParams(vmem_limit_bytes=20 * 2**20),
        cost_estimate=pl.CostEstimate(flops=10**9, bytes_accessed=4 * 10**6, transcendentals=10**6),
        name="slopes",
    )(place, scalars, rows, cols, row_ids, col_ids)


def text_products(side, place, rows, slopes, totals):
    half, width = slopes.shape[1] // 2, rows.shape[1]
    return pl.pallas_call(
        functools.partial(text_kernel, side),
        in_specs=[SMEM, VMEM, VMEM, VMEM],
        out_specs=VMEM,
        out_shape=jax.ShapeDtypeStruct((half + 8 * side, width), jnp.float32),
        compiler_params=pltpu.CompilerParams(vmem_limit_bytes=16 * 2**20),
        cost_estimate=pl.CostEstimate(flops=5 * 10**8, bytes_accessed=4 * 10**6, transcendentals=0),
        name="text_products_%d" % side,
    )(place, rows, slopes, totals)


def swap_sum(blocks, stats, axis):
    count, high, width = blocks.shape
    rider = jnp.concatenate(half_pieces(stats * (1 / 2048.0)) + [jnp.zeros((high - 3, 128), jnp.float16)], 0)
    rider = jnp.broadcast_to(rider[None], (count, high, 128))
    got = swap(jnp.concatenate([blocks, rider], 2), axis)
    stats = jnp.sum(got[:, :3, width:].astype(jnp.float32), (0, 1)).reshape(1, 128) * 2048.0
    return (jnp.sum(got[:, :, :width].astype(jnp.float32), 0), stats)


def half_pieces(value):
    pieces = []
    for _ in range(3):
        piece = lax.reduce_precision(value, 5, 10)
        pieces.append(piece.astype(jnp.float16))
        value = value - piece
    return pieces


def body(images, texts, image_ids, text_ids, log_scale, bias):
    width = images.shape[1]
    img_rows = images.shape[0]
    txt_rows = texts.shape[0]
    y, x, core = (lax.axis_index(a) for a in ("y", "x", "core"))
    z = lax.axis_index(Z)
    scale = jnp.exp(log_scale[0])
    copies, uyb, ux, rx, uy, ry = normalize(images, texts, lax.axis_size("y"))

    own = (swap(copies, "y").reshape(-1, width).astype(jnp.float32) * UNIT).astype(jnp.float16)
    cols = (uyb.astype(jnp.float32) * UNIT).astype(jnp.float16)
    cols = lax.all_gather(cols, Z + ("core",), axis=0, tiled=True)
    own, cols = lax.optimization_barrier((own, cols))
    rows = lax.all_gather(own, "x", axis=0, tiled=True)
    rows = (rows.astype(jnp.float32) * (1 / UNIT)).astype(jnp.bfloat16)
    cols = (cols.astype(jnp.float32) * (1 / UNIT)).astype(jnp.bfloat16)
    cols = cols.reshape(8, 2, txt_rows, width)
    mine = lax.dynamic_index_in_dim(cols, core, 1, keepdims=False)
    theirs = lax.dynamic_index_in_dim(cols, 1 - core, 1, keepdims=False)
    cols = jnp.concatenate([mine, theirs], 0).reshape(-1, width)

    col_ids = text_ids.reshape(8, 8, 4, 2, txt_rows)
    col_ids = lax.dynamic_index_in_dim(col_ids, y, 0, keepdims=False)
    col_ids = lax.dynamic_index_in_dim(col_ids, x, 1, keepdims=False)
    mine = lax.dynamic_index_in_dim(col_ids, core, 1, keepdims=False)
    theirs = lax.dynamic_index_in_dim(col_ids, 1 - core, 1, keepdims=False)
    col_ids = jnp.concatenate([mine, theirs], 0).reshape(1, -1)
    row_ids = image_ids.reshape(8, 8, 4, 2, img_rows)
    row_ids = lax.dynamic_index_in_dim(row_ids, z, 1, keepdims=False)
    row_ids = lax.dynamic_index_in_dim(row_ids, core, 2, keepdims=False)
    row_ids = row_ids.transpose(1, 0, 2).reshape(-1, 1)

    half = cols.shape[0] // 2
    high = rows.shape[0] // 4
    place = x.reshape(1).astype(jnp.int32)
    near, totals = slopes_of(place, jnp.stack([scale, bias[0]]), rows, cols, row_ids, col_ids)

    back = {}
    for k in (2, 1, 3, 0):
        drows = 64.0 * jnp.dot(near[k * high : (k + 1) * high], cols, preferred_element_type=jnp.float32)
        back[k] = drows.astype(jnp.float16) if k else drows
    for k in (2, 1, 3):
        back[k] = shifted(back[k], "x", k)

    got = shifted(text_products(1, place, rows, near, totals), "core", 1)
    mine = text_products(0, place, rows, near, totals)
    dcols = ((got[:half] + mine) * 32.0).astype(jnp.float16).reshape(8, txt_rows, width)
    dcols, stats = swap_sum(dcols, got[half : half + 1, :128] + totals[:1, :128], Z)
    stats = jnp.sum(spread(stats, "x"), 0)

    drows = sum(part.astype(jnp.float32) for part in back.values())
    drows = (drows * 0.25).astype(jnp.float16).reshape(8, -1, width)
    drows, stats = swap_sum(drows, stats, "y")
    stats = stats[0]

    total_texts = txt_rows * 512
    image_accum = drows * 0.0625
    text_accum = dcols * (1 / 32.0)
    image_grad = unnormalize(ux, rx[:, :1], scale * image_accum)
    text_grad = unnormalize(uy, ry[:, :1], scale * text_accum)
    lane = lax.iota(jnp.int32, stats.shape[0])
    stats = stats * jnp.where(lane == 1, scale, 1.0) * (1.0 / total_texts)
    loss, scale_grad, bias_grad = stats[0:1], stats[1:2], stats[2:3]
    return (image_grad, text_grad, loss, scale_grad, bias_grad)


def solution(mesh):
    fine = Mesh(mesh.devices.reshape(SIZES), AXES)
    split = P(AXES, None)
    return jax.shard_map(
        body,
        mesh=fine,
        in_specs=(split, split, P(), P(), P(), P()),
        out_specs=(split, split, P(), P(), P()),
        check_vma=False,
    )
```

```python
import functools

import jax
import jax.numpy as jnp
from jax import lax
from jax.experimental import pallas as pl
from jax.experimental.pallas import tpu as pltpu
from jax.sharding import Mesh, PartitionSpec as P

AXES = ("y", "zh", "zl", "x", "core")
SIZES = (8, 2, 4, 4, 2)
Z = ("zh", "zl")
UNIT = 16384.0


VMEM = pl.BlockSpec(memory_space=pltpu.VMEM)
SMEM = pl.BlockSpec(memory_space=pltpu.SMEM)


def normalize_kernel(rows, copies, unit, radius):
    values = rows[...].astype(jnp.float32)
    length = jnp.sqrt(jnp.sum(values * values, -1, keepdims=True) + 1e-06)
    values = values / length
    unit[...] = values
    radius[...] = jnp.broadcast_to(length, radius.shape)
    for i in range(copies.shape[0]):
        copies[i] = values.astype(jnp.bfloat16)


def normalize(rows, count):
    shapes = ((count,) + rows.shape, rows.shape, (rows.shape[0], 128))
    whole = lambda shape: pl.BlockSpec(shape, lambda i: (0,) * len(shape))
    types = (jnp.bfloat16, jnp.float32, jnp.float32)
    return pl.pallas_call(
        normalize_kernel,
        grid=(1,),
        in_specs=[whole(rows.shape)],
        out_specs=[whole(shape) for shape in shapes],
        out_shape=[jax.ShapeDtypeStruct(*pair) for pair in zip(shapes, types)],
        compiler_params=pltpu.CompilerParams(vmem_limit_bytes=8 * 2**20),
        cost_estimate=pl.CostEstimate(flops=10**6, bytes_accessed=10**6, transcendentals=1000),
        name="normalize_%d" % count,
    )(rows)


def unnormalize(unit, radius, grad):
    return (grad - unit * jnp.sum(unit * grad, -1, keepdims=True)) / radius


def swap(value, axis):
    return lax.all_to_all(value, axis, 0, 0, tiled=False)


def shifted(value, axis, steps):
    count = lax.axis_size(axis)
    return lax.ppermute(value, axis, [(i, (i + steps) % count) for i in range(count)])


def spread(block, axis):
    count = lax.axis_size(axis)
    return swap(jnp.broadcast_to(block[None], (count,) + block.shape), axis)


def slopes_kernel(place, scalars, rows, cols, row_ids, col_ids, slopes, totals):
    parts = 4
    high = rows.shape[0] // parts
    sums = [0.0, 0.0, 0.0]
    for k in range(parts):
        part = pl.ds(pl.multiple_of(lax.rem(place[0] + k, parts) * high, high), high)
        dots = lax.dot_general(
            rows[part, :], cols[...], (((1,), (1,)), ((), ())), preferred_element_type=jnp.float32
        )
        logits = scalars[0] * dots + scalars[1]
        match = row_ids[part, :] == col_ids[...]
        against = jnp.where(match, -logits, logits)
        decay = jnp.exp(-jnp.abs(against))
        objective = jnp.maximum(against, 0.0) + jnp.log1p(decay)
        weight = jnp.where(against >= 0.0, 1.0, decay) / (1.0 + decay)
        slope = jnp.where(match, -weight, weight)
        slopes[k * high : (k + 1) * high, :] = slope.astype(jnp.bfloat16)
        for i, term in enumerate((objective, slope * dots, slope)):
            sums[i] += jnp.sum(term, 0, keepdims=True)
    lane = lax.broadcasted_iota(jnp.int32, totals.shape, 1)
    total = jnp.zeros(totals.shape, jnp.float32)
    for i in range(3):
        total = jnp.where(lane == i, jnp.sum(sums[i], 1, keepdims=True), total)
    totals[...] = total


def text_kernel(side, place, rows, slopes, totals, out):
    parts = 4
    high = rows.shape[0] // parts
    half = slopes.shape[1] // 2
    for k in range(parts):
        part = pl.ds(pl.multiple_of(lax.rem(place[0] + k, parts) * high, high), high)
        product = lax.dot_general(
            slopes[k * high : (k + 1) * high, side * half : (side + 1) * half],
            rows[part, :],
            (((0,), (0,)), ((), ())),
            preferred_element_type=jnp.float32,
        )
        out[:half, :] = product if k == 0 else out[:half, :] + product
    if side:
        out[half:, :] = totals[...]


def slopes_of(place, scalars, rows, cols, row_ids, col_ids):
    wide, width = cols.shape
    return pl.pallas_call(
        slopes_kernel,
        in_specs=[SMEM, SMEM, VMEM, VMEM, VMEM, VMEM],
        out_specs=[VMEM, VMEM],
        out_shape=(
            jax.ShapeDtypeStruct((rows.shape[0], wide), jnp.bfloat16),
            jax.ShapeDtypeStruct((8, width), jnp.float32),
        ),
        compiler_params=pltpu.CompilerParams(vmem_limit_bytes=20 * 2**20),
        cost_estimate=pl.CostEstimate(flops=10**9, bytes_accessed=4 * 10**6, transcendentals=10**6),
        name="slopes",
    )(place, scalars, rows, cols, row_ids, col_ids)


def text_products(side, place, rows, slopes, totals):
    half, width = slopes.shape[1] // 2, rows.shape[1]
    return pl.pallas_call(
        functools.partial(text_kernel, side),
        in_specs=[SMEM, VMEM, VMEM, VMEM],
        out_specs=VMEM,
        out_shape=jax.ShapeDtypeStruct((half + 8 * side, width), jnp.float32),
        compiler_params=pltpu.CompilerParams(vmem_limit_bytes=16 * 2**20),
        cost_estimate=pl.CostEstimate(flops=5 * 10**8, bytes_accessed=4 * 10**6, transcendentals=0),
        name="text_products_%d" % side,
    )(place, rows, slopes, totals)


def swap_sum(blocks, stats, axis):
    count, high, width = blocks.shape
    rider = jnp.concatenate(half_pieces(stats * (1 / 2048.0)) + [jnp.zeros((high - 3, 128), jnp.float16)], 0)
    rider = jnp.broadcast_to(rider[None], (count, high, 128))
    got = swap(jnp.concatenate([blocks, rider], 2), axis)
    stats = jnp.sum(got[:, :3, width:].astype(jnp.float32), (0, 1)).reshape(1, 128) * 2048.0
    return (jnp.sum(got[:, :, :width].astype(jnp.float32), 0), stats)


def half_pieces(value):
    pieces = []
    for _ in range(3):
        piece = lax.reduce_precision(value, 5, 10)
        pieces.append(piece.astype(jnp.float16))
        value = value - piece
    return pieces


def body(images, texts, image_ids, text_ids, log_scale, bias):
    width = images.shape[1]
    img_rows = images.shape[0]
    txt_rows = texts.shape[0]
    y, x, core = (lax.axis_index(a) for a in ("y", "x", "core"))
    z = lax.axis_index(Z)
    scale = jnp.exp(log_scale[0])
    copies, ux, rx = normalize(images, lax.axis_size("y"))
    uyb, uy, ry = normalize(texts, 1)

    own = swap(copies, "y").reshape(-1, width)
    cols = (uyb[0].astype(jnp.float32) * UNIT).astype(jnp.float16)
    own, cols = lax.optimization_barrier((own, cols))
    rows = spread(own, "x").reshape(-1, width)
    cols = lax.all_gather(cols, Z + ("core",), axis=0, tiled=True)
    cols = (cols.astype(jnp.float32) * (1 / UNIT)).astype(jnp.bfloat16)
    cols = cols.reshape(8, 2, txt_rows, width)
    mine = lax.dynamic_index_in_dim(cols, core, 1, keepdims=False)
    theirs = lax.dynamic_index_in_dim(cols, 1 - core, 1, keepdims=False)
    cols = jnp.concatenate([mine, theirs], 0).reshape(-1, width)

    col_ids = text_ids.reshape(8, 8, 4, 2, txt_rows)
    col_ids = lax.dynamic_index_in_dim(col_ids, y, 0, keepdims=False)
    col_ids = lax.dynamic_index_in_dim(col_ids, x, 1, keepdims=False)
    mine = lax.dynamic_index_in_dim(col_ids, core, 1, keepdims=False)
    theirs = lax.dynamic_index_in_dim(col_ids, 1 - core, 1, keepdims=False)
    col_ids = jnp.concatenate([mine, theirs], 0).reshape(1, -1)
    row_ids = image_ids.reshape(8, 8, 4, 2, img_rows)
    row_ids = lax.dynamic_index_in_dim(row_ids, z, 1, keepdims=False)
    row_ids = lax.dynamic_index_in_dim(row_ids, core, 2, keepdims=False)
    row_ids = row_ids.transpose(1, 0, 2).reshape(-1, 1)

    half = cols.shape[0] // 2
    high = rows.shape[0] // 4
    place = x.reshape(1).astype(jnp.int32)
    near, totals = slopes_of(place, jnp.stack([scale, bias[0]]), rows, cols, row_ids, col_ids)

    back = {}
    for k in (2, 1, 3, 0):
        drows = 64.0 * jnp.dot(near[k * high : (k + 1) * high], cols, preferred_element_type=jnp.float32)
        back[k] = drows.astype(jnp.float16) if k else drows

    got = shifted(text_products(1, place, rows, near, totals), "core", 1)
    mine = text_products(0, place, rows, near, totals)
    dcols = ((got[:half] + mine) * 32.0).astype(jnp.float16).reshape(8, txt_rows, width)
    dcols, back[1], back[2], back[3] = lax.optimization_barrier((dcols, back[1], back[2], back[3]))
    dcols, stats = swap_sum(dcols, got[half : half + 1, :128] + totals[:1, :128], Z)
    stats = jnp.sum(spread(stats, "x"), 0)

    back[0] = lax.optimization_barrier(back[0])
    for k in (2, 1, 3):
        back[k] = shifted(back[k], "x", k)
    drows = sum(part.astype(jnp.float32) for part in back.values())
    drows = (drows * 0.25).astype(jnp.float16).reshape(8, -1, width)
    drows, stats = swap_sum(drows, stats, "y")
    stats = stats[0]

    total_texts = txt_rows * 512
    image_accum = drows * 0.0625
    text_accum = dcols * (1 / 32.0)
    image_grad = unnormalize(ux, rx[:, :1], scale * image_accum)
    text_grad = unnormalize(uy, ry[:, :1], scale * text_accum)
    lane = lax.iota(jnp.int32, stats.shape[0])
    stats = stats * jnp.where(lane == 1, scale, 1.0) * (1.0 / total_texts)
    loss, scale_grad, bias_grad = stats[0:1], stats[1:2], stats[2:3]
    return (image_grad, text_grad, loss, scale_grad, bias_grad)


def solution(mesh):
    fine = Mesh(mesh.devices.reshape(SIZES), AXES)
    split = P(AXES, None)
    return jax.shard_map(
        body,
        mesh=fine,
        in_specs=(split, split, P(), P(), P(), P()),
        out_specs=(split, split, P(), P(), P()),
        check_vma=False,
    )
```

```python
import functools

import jax
import jax.numpy as jnp
from jax import lax
from jax.experimental import pallas as pl
from jax.experimental.pallas import tpu as pltpu
from jax.sharding import Mesh, PartitionSpec as P

AXES = ("y", "zh", "zl", "x", "core")
SIZES = (8, 2, 4, 4, 2)
Z = ("zh", "zl")
UNIT = 16384.0


VMEM = pl.BlockSpec(memory_space=pltpu.VMEM)
SMEM = pl.BlockSpec(memory_space=pltpu.SMEM)


def normalize_kernel(rows, copies, unit, radius):
    values = rows[...].astype(jnp.float32)
    length = jnp.sqrt(jnp.sum(values * values, -1, keepdims=True) + 1e-06)
    values = values / length
    unit[...] = values
    radius[...] = jnp.broadcast_to(length, radius.shape)
    for i in range(copies.shape[0]):
        copies[i] = values.astype(jnp.bfloat16)


def normalize(rows, count):
    shapes = ((count,) + rows.shape, rows.shape, (rows.shape[0], 128))
    whole = lambda shape: pl.BlockSpec(shape, lambda i: (0,) * len(shape))
    types = (jnp.bfloat16, jnp.float32, jnp.float32)
    return pl.pallas_call(
        normalize_kernel,
        grid=(1,),
        in_specs=[whole(rows.shape)],
        out_specs=[whole(shape) for shape in shapes],
        out_shape=[jax.ShapeDtypeStruct(*pair) for pair in zip(shapes, types)],
        compiler_params=pltpu.CompilerParams(vmem_limit_bytes=8 * 2**20),
        cost_estimate=pl.CostEstimate(flops=10**6, bytes_accessed=10**6, transcendentals=1000),
        name="normalize_%d" % count,
    )(rows)


def unnormalize(unit, radius, grad):
    return (grad - unit * jnp.sum(unit * grad, -1, keepdims=True)) / radius


def swap(value, axis):
    return lax.all_to_all(value, axis, 0, 0, tiled=False)


def shifted(value, axis, steps):
    count = lax.axis_size(axis)
    return lax.ppermute(value, axis, [(i, (i + steps) % count) for i in range(count)])


def spread(block, axis):
    count = lax.axis_size(axis)
    return swap(jnp.broadcast_to(block[None], (count,) + block.shape), axis)


def slopes_kernel(place, scalars, rows, cols, row_ids, col_ids, slopes, totals):
    parts = 4
    high = rows.shape[0] // parts
    sums = [0.0, 0.0, 0.0]
    ones = jnp.ones((row_ids.shape[1], cols.shape[0]), jnp.bfloat16)
    for k in range(parts):
        part = pl.ds(pl.multiple_of(lax.rem(place[0] + k, parts) * high, high), high)
        dots = lax.dot_general(
            rows[part, :], cols[...], (((1,), (1,)), ((), ())), preferred_element_type=jnp.float32
        )
        logits = scalars[0] * dots + scalars[1]
        spot = lax.dot_general(
            row_ids[lax.rem(place[0] + k, parts)], ones, (((0,), (0,)), ((), ())), preferred_element_type=jnp.float32
        )
        match = spot == col_ids[...]
        against = jnp.where(match, -logits, logits)
        decay = jnp.exp(-jnp.abs(against))
        objective = jnp.maximum(against, 0.0) + jnp.log1p(decay)
        weight = jnp.where(against >= 0.0, 1.0, decay) / (1.0 + decay)
        slope = jnp.where(match, -weight, weight)
        slopes[k * high : (k + 1) * high, :] = slope.astype(jnp.bfloat16)
        for i, term in enumerate((objective, slope * dots, slope)):
            sums[i] += jnp.sum(term, 0, keepdims=True)
    lane = lax.broadcasted_iota(jnp.int32, totals.shape, 1)
    total = jnp.zeros(totals.shape, jnp.float32)
    for i in range(3):
        total = jnp.where(lane == i, jnp.sum(sums[i], 1, keepdims=True), total)
    totals[...] = total


def text_kernel(side, place, rows, slopes, totals, out):
    parts = 4
    high = rows.shape[0] // parts
    half = slopes.shape[1] // 2
    for k in range(parts):
        part = pl.ds(pl.multiple_of(lax.rem(place[0] + k, parts) * high, high), high)
        product = lax.dot_general(
            slopes[k * high : (k + 1) * high, side * half : (side + 1) * half],
            rows[part, :],
            (((0,), (0,)), ((), ())),
            preferred_element_type=jnp.float32,
        )
        out[:half, :] = product if k == 0 else out[:half, :] + product
    if side:
        out[half:, :] = totals[...]


def slopes_of(place, scalars, rows, cols, row_ids, col_ids):
    wide, width = cols.shape
    return pl.pallas_call(
        slopes_kernel,
        in_specs=[SMEM, SMEM, VMEM, VMEM, VMEM, VMEM],
        out_specs=[VMEM, VMEM],
        out_shape=(
            jax.ShapeDtypeStruct((rows.shape[0], wide), jnp.bfloat16),
            jax.ShapeDtypeStruct((8, width), jnp.float32),
        ),
        compiler_params=pltpu.CompilerParams(vmem_limit_bytes=20 * 2**20),
        cost_estimate=pl.CostEstimate(flops=10**9, bytes_accessed=4 * 10**6, transcendentals=10**6),
        name="slopes",
    )(place, scalars, rows, cols, row_ids, col_ids)


def text_products(side, place, rows, slopes, totals):
    half, width = slopes.shape[1] // 2, rows.shape[1]
    return pl.pallas_call(
        functools.partial(text_kernel, side),
        in_specs=[SMEM, VMEM, VMEM, VMEM],
        out_specs=VMEM,
        out_shape=jax.ShapeDtypeStruct((half + 8 * side, width), jnp.float32),
        compiler_params=pltpu.CompilerParams(vmem_limit_bytes=16 * 2**20),
        cost_estimate=pl.CostEstimate(flops=5 * 10**8, bytes_accessed=4 * 10**6, transcendentals=0),
        name="text_products_%d" % side,
    )(place, rows, slopes, totals)


def swap_sum(blocks, stats, axis):
    count, high, width = blocks.shape
    rider = jnp.concatenate(half_pieces(stats * (1 / 2048.0)) + [jnp.zeros((high - 3, 128), jnp.float16)], 0)
    rider = jnp.broadcast_to(rider[None], (count, high, 128))
    got = swap(jnp.concatenate([blocks, rider], 2), axis)
    stats = jnp.sum(got[:, :3, width:].astype(jnp.float32), (0, 1)).reshape(1, 128) * 2048.0
    return (jnp.sum(got[:, :, :width].astype(jnp.float32), 0), stats)


def half_pieces(value):
    pieces = []
    for _ in range(3):
        piece = lax.reduce_precision(value, 5, 10)
        pieces.append(piece.astype(jnp.float16))
        value = value - piece
    return pieces


def body(images, texts, image_ids, text_ids, log_scale, bias):
    width = images.shape[1]
    img_rows = images.shape[0]
    txt_rows = texts.shape[0]
    y, x, core = (lax.axis_index(a) for a in ("y", "x", "core"))
    z = lax.axis_index(Z)
    scale = jnp.exp(log_scale[0])
    copies, ux, rx = normalize(images, lax.axis_size("y"))
    uyb, uy, ry = normalize(texts, 1)

    own = swap(copies, "y").reshape(-1, width)
    cols = (uyb[0].astype(jnp.float32) * UNIT).astype(jnp.float16)
    own, cols = lax.optimization_barrier((own, cols))
    rows = spread(own, "x").reshape(-1, width)
    cols = lax.all_gather(cols, Z + ("core",), axis=0, tiled=True)
    cols = (cols.astype(jnp.float32) * (1 / UNIT)).astype(jnp.bfloat16)
    cols = cols.reshape(8, 2, txt_rows, width)
    mine = lax.dynamic_index_in_dim(cols, core, 1, keepdims=False)
    theirs = lax.dynamic_index_in_dim(cols, 1 - core, 1, keepdims=False)
    cols = jnp.concatenate([mine, theirs], 0).reshape(-1, width)

    col_ids = text_ids.reshape(8, 8, 4, 2, txt_rows)
    col_ids = lax.dynamic_index_in_dim(col_ids, y, 0, keepdims=False)
    col_ids = lax.dynamic_index_in_dim(col_ids, x, 1, keepdims=False)
    mine = lax.dynamic_index_in_dim(col_ids, core, 1, keepdims=False)
    theirs = lax.dynamic_index_in_dim(col_ids, 1 - core, 1, keepdims=False)
    col_ids = jnp.concatenate([mine, theirs], 0).reshape(1, -1).astype(jnp.float32)
    row_ids = image_ids.reshape(8, 8, 4, 2, img_rows)
    row_ids = lax.dynamic_index_in_dim(row_ids, z, 1, keepdims=False)
    row_ids = lax.dynamic_index_in_dim(row_ids, core, 2, keepdims=False)
    row_ids = row_ids.transpose(1, 0, 2).reshape(4, 1, -1)
    row_ids = jnp.concatenate([row_ids & -128, row_ids & 127, jnp.zeros((4, 6, 8 * img_rows), jnp.int32)], 1)
    row_ids = row_ids.astype(jnp.bfloat16)

    half = cols.shape[0] // 2
    high = rows.shape[0] // 4
    place = x.reshape(1).astype(jnp.int32)
    near, totals = slopes_of(place, jnp.stack([scale, bias[0]]), rows, cols, row_ids, col_ids)

    back = {}
    for k in (2, 1, 3, 0):
        drows = 64.0 * jnp.dot(near[k * high : (k + 1) * high], cols, preferred_element_type=jnp.float32)
        back[k] = drows.astype(jnp.float16) if k else drows

    got = shifted(text_products(1, place, rows, near, totals), "core", 1)
    mine = text_products(0, place, rows, near, totals)
    dcols = ((got[:half] + mine) * 32.0).astype(jnp.float16).reshape(8, txt_rows, width)
    dcols, back[1], back[2], back[3] = lax.optimization_barrier((dcols, back[1], back[2], back[3]))
    dcols, stats = swap_sum(dcols, got[half : half + 1, :128] + totals[:1, :128], Z)
    stats = jnp.sum(spread(stats, "x"), 0)

    for k in (2, 1, 3):
        back[k] = shifted(back[k], "x", k)
    drows = sum(part.astype(jnp.float32) for part in back.values())
    drows = (drows * 0.25).astype(jnp.float16).reshape(8, -1, width)
    drows, stats = swap_sum(drows, stats, "y")
    stats = stats[0]

    total_texts = txt_rows * 512
    image_accum = drows * 0.0625
    text_accum = dcols * (1 / 32.0)
    image_grad = unnormalize(ux, rx[:, :1], scale * image_accum)
    text_grad = unnormalize(uy, ry[:, :1], scale * text_accum)
    lane = lax.iota(jnp.int32, stats.shape[0])
    stats = stats * jnp.where(lane == 1, scale, 1.0) * (1.0 / total_texts)
    loss, scale_grad, bias_grad = stats[0:1], stats[1:2], stats[2:3]
    return (image_grad, text_grad, loss, scale_grad, bias_grad)


def solution(mesh):
    fine = Mesh(mesh.devices.reshape(SIZES), AXES)
    split = P(AXES, None)
    return jax.shard_map(
        body,
        mesh=fine,
        in_specs=(split, split, P(), P(), P(), P()),
        out_specs=(split, split, P(), P(), P()),
        check_vma=False,
    )
```

```python
import functools

import jax
import jax.numpy as jnp
from jax import lax
from jax.experimental import pallas as pl
from jax.experimental.pallas import tpu as pltpu
from jax.sharding import Mesh, PartitionSpec as P

AXES = ("y", "zh", "zl", "x", "core")
SIZES = (8, 2, 4, 4, 2)
Z = ("zh", "zl")
UNIT = 16384.0


VMEM = pl.BlockSpec(memory_space=pltpu.VMEM)
SMEM = pl.BlockSpec(memory_space=pltpu.SMEM)


def normalize_kernel(rows, copies, unit, radius):
    values = rows[...].astype(jnp.float32)
    length = jnp.sqrt(jnp.sum(values * values, -1, keepdims=True) + 1e-06)
    values = values / length
    unit[...] = values
    radius[...] = jnp.broadcast_to(length, radius.shape)
    for i in range(copies.shape[0]):
        copies[i] = values.astype(jnp.bfloat16)


def normalize(rows, count):
    shapes = ((count,) + rows.shape, rows.shape, (rows.shape[0], 128))
    whole = lambda shape: pl.BlockSpec(shape, lambda i: (0,) * len(shape))
    types = (jnp.bfloat16, jnp.float32, jnp.float32)
    return pl.pallas_call(
        normalize_kernel,
        grid=(1,),
        in_specs=[whole(rows.shape)],
        out_specs=[whole(shape) for shape in shapes],
        out_shape=[jax.ShapeDtypeStruct(*pair) for pair in zip(shapes, types)],
        compiler_params=pltpu.CompilerParams(vmem_limit_bytes=8 * 2**20),
        cost_estimate=pl.CostEstimate(flops=10**6, bytes_accessed=10**6, transcendentals=1000),
        name="normalize_%d" % count,
    )(rows)


def unnormalize(unit, radius, grad):
    return (grad - unit * jnp.sum(unit * grad, -1, keepdims=True)) / radius


def swap(value, axis):
    return lax.all_to_all(value, axis, 0, 0, tiled=False)


def shifted(value, axis, steps):
    count = lax.axis_size(axis)
    return lax.ppermute(value, axis, [(i, (i + steps) % count) for i in range(count)])


def spread(block, axis):
    count = lax.axis_size(axis)
    return swap(jnp.broadcast_to(block[None], (count,) + block.shape), axis)


def slopes_kernel(place, scalars, rows, cols, row_ids, col_ids, slopes, totals):
    parts = 4
    high = rows.shape[0] // parts
    sums = [0.0, 0.0, 0.0]
    ones = jnp.ones((row_ids.shape[1], cols.shape[0]), jnp.bfloat16)
    for k in range(parts):
        part = pl.ds(pl.multiple_of(lax.rem(place[0] + k, parts) * high, high), high)
        dots = lax.dot_general(
            rows[part, :], cols[...], (((1,), (1,)), ((), ())), preferred_element_type=jnp.float32
        )
        logits = scalars[0] * dots + scalars[1]
        spot = lax.dot_general(
            row_ids[lax.rem(place[0] + k, parts)], ones, (((0,), (0,)), ((), ())), preferred_element_type=jnp.float32
        )
        match = spot == col_ids[...]
        against = jnp.where(match, -logits, logits)
        decay = jnp.exp(-jnp.abs(against))
        objective = jnp.maximum(against, 0.0) + jnp.log1p(decay)
        weight = jnp.where(against >= 0.0, 1.0, decay) / (1.0 + decay)
        slope = jnp.where(match, -weight, weight)
        slopes[k * high : (k + 1) * high, :] = slope.astype(jnp.bfloat16)
        for i, term in enumerate((objective, slope * dots, slope)):
            sums[i] += jnp.sum(term, 0, keepdims=True)
    lane = lax.broadcasted_iota(jnp.int32, totals.shape, 1)
    total = jnp.zeros(totals.shape, jnp.float32)
    for i in range(3):
        total = jnp.where(lane == i, jnp.sum(sums[i], 1, keepdims=True), total)
    totals[...] = total


def text_kernel(side, place, rows, slopes, totals, out):
    parts = 4
    high = rows.shape[0] // parts
    half = slopes.shape[1] // 2
    for k in range(parts):
        part = pl.ds(pl.multiple_of(lax.rem(place[0] + k, parts) * high, high), high)
        product = lax.dot_general(
            slopes[k * high : (k + 1) * high, side * half : (side + 1) * half],
            rows[part, :],
            (((0,), (0,)), ((), ())),
            preferred_element_type=jnp.float32,
        )
        out[:half, :] = product if k == 0 else out[:half, :] + product
    if side:
        out[half:, :] = totals[...]


def slopes_of(place, scalars, rows, cols, row_ids, col_ids):
    wide, width = cols.shape
    return pl.pallas_call(
        slopes_kernel,
        in_specs=[SMEM, SMEM, VMEM, VMEM, VMEM, VMEM],
        out_specs=[VMEM, VMEM],
        out_shape=(
            jax.ShapeDtypeStruct((rows.shape[0], wide), jnp.bfloat16),
            jax.ShapeDtypeStruct((8, width), jnp.float32),
        ),
        compiler_params=pltpu.CompilerParams(vmem_limit_bytes=20 * 2**20),
        cost_estimate=pl.CostEstimate(flops=10**9, bytes_accessed=4 * 10**6, transcendentals=10**6),
        name="slopes",
    )(place, scalars, rows, cols, row_ids, col_ids)


def text_products(side, place, rows, slopes, totals):
    half, width = slopes.shape[1] // 2, rows.shape[1]
    return pl.pallas_call(
        functools.partial(text_kernel, side),
        in_specs=[SMEM, VMEM, VMEM, VMEM],
        out_specs=VMEM,
        out_shape=jax.ShapeDtypeStruct((half + 8 * side, width), jnp.float32),
        compiler_params=pltpu.CompilerParams(vmem_limit_bytes=16 * 2**20),
        cost_estimate=pl.CostEstimate(flops=5 * 10**8, bytes_accessed=4 * 10**6, transcendentals=0),
        name="text_products_%d" % side,
    )(place, rows, slopes, totals)


def finish_kernel(last, scale, unit, radius, accum, sums, grad, loss, scale_grad, bias_grad):
    values = unit[...]
    total = accum[...] * (scale[0] * last[0])
    grad[...] = (total - values * jnp.sum(values * total, -1, keepdims=True)) / radius[:, :1]
    loss[0] = sums[0, 0] * last[1]
    scale_grad[0] = sums[0, 1] * (scale[0] * last[1])
    bias_grad[0] = sums[0, 2] * last[1]


def finish(last, scale, unit, radius, accum, sums):
    one = jax.ShapeDtypeStruct((1,), jnp.float32)
    return pl.pallas_call(
        functools.partial(finish_kernel, last),
        in_specs=[SMEM, VMEM, VMEM, VMEM, VMEM],
        out_specs=[VMEM, SMEM, SMEM, SMEM],
        out_shape=[jax.ShapeDtypeStruct(unit.shape, jnp.float32), one, one, one],
        compiler_params=pltpu.CompilerParams(vmem_limit_bytes=8 * 2**20),
        cost_estimate=pl.CostEstimate(flops=10**6, bytes_accessed=10**6, transcendentals=0),
        name="finish",
    )(scale.reshape(1), unit, radius, accum, sums)


def swap_sum(blocks, stats, axis):
    count, high, width = blocks.shape
    rider = jnp.concatenate(half_pieces(stats * (1 / 2048.0)) + [jnp.zeros((high - 3, 128), jnp.float16)], 0)
    rider = jnp.broadcast_to(rider[None], (count, high, 128))
    got = swap(jnp.concatenate([blocks, rider], 2), axis)
    stats = jnp.sum(got[:, :3, width:].astype(jnp.float32), (0, 1)).reshape(1, 128) * 2048.0
    return (jnp.sum(got[:, :, :width].astype(jnp.float32), 0), stats)


def half_pieces(value):
    pieces = []
    for _ in range(3):
        piece = lax.reduce_precision(value, 5, 10)
        pieces.append(piece.astype(jnp.float16))
        value = value - piece
    return pieces


def body(images, texts, image_ids, text_ids, log_scale, bias):
    width = images.shape[1]
    img_rows = images.shape[0]
    txt_rows = texts.shape[0]
    y, x, core = (lax.axis_index(a) for a in ("y", "x", "core"))
    z = lax.axis_index(Z)
    scale = jnp.exp(log_scale[0])
    copies, ux, rx = normalize(images, lax.axis_size("y"))
    uyb, uy, ry = normalize(texts, 1)

    own = swap(copies, "y").reshape(-1, width)
    cols = (uyb[0].astype(jnp.float32) * UNIT).astype(jnp.float16)
    own, cols = lax.optimization_barrier((own, cols))
    rows = spread(own, "x").reshape(-1, width)
    cols = lax.all_gather(cols, Z + ("core",), axis=0, tiled=True)
    cols = (cols.astype(jnp.float32) * (1 / UNIT)).astype(jnp.bfloat16)
    cols = cols.reshape(8, 2, txt_rows, width)
    mine = lax.dynamic_index_in_dim(cols, core, 1, keepdims=False)
    theirs = lax.dynamic_index_in_dim(cols, 1 - core, 1, keepdims=False)
    cols = jnp.concatenate([mine, theirs], 0).reshape(-1, width)

    col_ids = text_ids.reshape(8, 8, 4, 2, txt_rows)
    col_ids = lax.dynamic_index_in_dim(col_ids, y, 0, keepdims=False)
    col_ids = lax.dynamic_index_in_dim(col_ids, x, 1, keepdims=False)
    mine = lax.dynamic_index_in_dim(col_ids, core, 1, keepdims=False)
    theirs = lax.dynamic_index_in_dim(col_ids, 1 - core, 1, keepdims=False)
    col_ids = jnp.concatenate([mine, theirs], 0).reshape(1, -1).astype(jnp.float32)
    row_ids = image_ids.reshape(8, 8, 4, 2, img_rows)
    row_ids = lax.dynamic_index_in_dim(row_ids, z, 1, keepdims=False)
    row_ids = lax.dynamic_index_in_dim(row_ids, core, 2, keepdims=False)
    row_ids = row_ids.transpose(1, 0, 2).reshape(4, 1, -1)
    row_ids = jnp.concatenate([row_ids & -128, row_ids & 127, jnp.zeros((4, 6, 8 * img_rows), jnp.int32)], 1)
    row_ids = row_ids.astype(jnp.bfloat16)

    half = cols.shape[0] // 2
    high = rows.shape[0] // 4
    place = x.reshape(1).astype(jnp.int32)
    near, totals = slopes_of(place, jnp.stack([scale, bias[0]]), rows, cols, row_ids, col_ids)

    back = {}
    for k in (2, 1, 3, 0):
        drows = 64.0 * jnp.dot(near[k * high : (k + 1) * high], cols, preferred_element_type=jnp.float32)
        back[k] = drows.astype(jnp.float16) if k else drows

    got = shifted(text_products(1, place, rows, near, totals), "core", 1)
    mine = text_products(0, place, rows, near, totals)
    dcols = ((got[:half] + mine) * 32.0).astype(jnp.float16).reshape(8, txt_rows, width)
    dcols, back[1], back[2], back[3] = lax.optimization_barrier((dcols, back[1], back[2], back[3]))
    dcols, stats = swap_sum(dcols, got[half : half + 1, :128] + totals[:1, :128], Z)
    stats = jnp.sum(spread(stats, "x"), 0)

    for k in (2, 1, 3):
        back[k] = shifted(back[k], "x", k)
    drows = sum(part.astype(jnp.float32) for part in back.values())
    drows = (drows * 0.25).astype(jnp.float16).reshape(8, -1, width)
    drows, stats = swap_sum(drows, stats, "y")
    text_grad = unnormalize(uy, ry[:, :1], scale * (dcols * (1 / 32.0)))
    image_grad, loss, scale_grad, bias_grad = finish(
        (0.0625, 1.0 / (txt_rows * 512)), scale, ux, rx, drows, stats
    )
    return (image_grad, text_grad, loss, scale_grad, bias_grad)


def solution(mesh):
    fine = Mesh(mesh.devices.reshape(SIZES), AXES)
    split = P(AXES, None)
    return jax.shard_map(
        body,
        mesh=fine,
        in_specs=(split, split, P(), P(), P(), P()),
        out_specs=(split, split, P(), P(), P()),
        check_vma=False,
    )
```

```python
import functools

import jax
import jax.numpy as jnp
from jax import lax
from jax.experimental import pallas as pl
from jax.experimental.pallas import tpu as pltpu
from jax.sharding import Mesh, PartitionSpec as P

AXES = ("y", "zh", "zl", "x", "core")
SIZES = (8, 2, 4, 4, 2)
Z = ("zh", "zl")
UNIT = 16384.0


VMEM = pl.BlockSpec(memory_space=pltpu.VMEM)
SMEM = pl.BlockSpec(memory_space=pltpu.SMEM)


def normalize_kernel(rows, copies, unit, radius):
    values = rows[...].astype(jnp.float32)
    length = jnp.sqrt(jnp.sum(values * values, -1, keepdims=True) + 1e-06)
    values = values / length
    unit[...] = values
    radius[...] = jnp.broadcast_to(length, radius.shape)
    for i in range(copies.shape[0]):
        copies[i] = values.astype(jnp.bfloat16)


def normalize(rows, count):
    shapes = ((count,) + rows.shape, rows.shape, (rows.shape[0], 128))
    whole = lambda shape: pl.BlockSpec(shape, lambda i: (0,) * len(shape))
    types = (jnp.bfloat16, jnp.float32, jnp.float32)
    return pl.pallas_call(
        normalize_kernel,
        grid=(1,),
        in_specs=[whole(rows.shape)],
        out_specs=[whole(shape) for shape in shapes],
        out_shape=[jax.ShapeDtypeStruct(*pair) for pair in zip(shapes, types)],
        compiler_params=pltpu.CompilerParams(vmem_limit_bytes=8 * 2**20),
        cost_estimate=pl.CostEstimate(flops=10**6, bytes_accessed=10**6, transcendentals=1000),
        name="normalize_%d" % count,
    )(rows)


def unnormalize(unit, radius, grad):
    return (grad - unit * jnp.sum(unit * grad, -1, keepdims=True)) / radius


def swap(value, axis):
    return lax.all_to_all(value, axis, 0, 0, tiled=False)


def shifted(value, axis, steps):
    count = lax.axis_size(axis)
    return lax.ppermute(value, axis, [(i, (i + steps) % count) for i in range(count)])


def spread(block, axis):
    count = lax.axis_size(axis)
    return swap(jnp.broadcast_to(block[None], (count,) + block.shape), axis)


def slopes_kernel(place, scalars, rows, cols, row_ids, col_ids, slopes, totals):
    parts = 4
    high = rows.shape[0] // parts
    sums = [0.0, 0.0, 0.0]
    ones = jnp.ones((row_ids.shape[1], cols.shape[0]), jnp.bfloat16)
    for k in range(parts):
        part = pl.ds(pl.multiple_of(lax.rem(place[0] + k, parts) * high, high), high)
        dots = lax.dot_general(
            rows[part, :], cols[...], (((1,), (1,)), ((), ())), preferred_element_type=jnp.float32
        )
        logits = scalars[0] * dots + scalars[1]
        spot = lax.dot_general(
            row_ids[lax.rem(place[0] + k, parts)], ones, (((0,), (0,)), ((), ())), preferred_element_type=jnp.float32
        )
        match = spot == col_ids[...]
        against = jnp.where(match, -logits, logits)
        decay = jnp.exp(-jnp.abs(against))
        objective = jnp.maximum(against, 0.0) + jnp.log1p(decay)
        weight = jnp.where(against >= 0.0, 1.0, decay) / (1.0 + decay)
        slope = jnp.where(match, -weight, weight)
        slopes[k * high : (k + 1) * high, :] = slope.astype(jnp.bfloat16)
        for i, term in enumerate((objective, slope * dots, slope)):
            sums[i] += jnp.sum(term, 0, keepdims=True)
    lane = lax.broadcasted_iota(jnp.int32, totals.shape, 1)
    total = jnp.zeros(totals.shape, jnp.float32)
    for i in range(3):
        total = jnp.where(lane == i, jnp.sum(sums[i], 1, keepdims=True), total)
    totals[...] = total


def text_kernel(side, place, rows, slopes, totals, out):
    parts = 4
    high = rows.shape[0] // parts
    half = slopes.shape[1] // 2
    for k in range(parts):
        part = pl.ds(pl.multiple_of(lax.rem(place[0] + k, parts) * high, high), high)
        product = lax.dot_general(
            slopes[k * high : (k + 1) * high, side * half : (side + 1) * half],
            rows[part, :],
            (((0,), (0,)), ((), ())),
            preferred_element_type=jnp.float32,
        )
        out[:half, :] = product if k == 0 else out[:half, :] + product
    if side:
        out[half:, :] = totals[...]


def slopes_of(place, scalars, rows, cols, row_ids, col_ids):
    wide, width = cols.shape
    return pl.pallas_call(
        slopes_kernel,
        in_specs=[SMEM, SMEM, VMEM, VMEM, VMEM, VMEM],
        out_specs=[VMEM, VMEM],
        out_shape=(
            jax.ShapeDtypeStruct((rows.shape[0], wide), jnp.bfloat16),
            jax.ShapeDtypeStruct((8, width), jnp.float32),
        ),
        compiler_params=pltpu.CompilerParams(vmem_limit_bytes=20 * 2**20),
        cost_estimate=pl.CostEstimate(flops=10**9, bytes_accessed=4 * 10**6, transcendentals=10**6),
        name="slopes",
    )(place, scalars, rows, cols, row_ids, col_ids)


def text_products(side, place, rows, slopes, totals):
    half, width = slopes.shape[1] // 2, rows.shape[1]
    return pl.pallas_call(
        functools.partial(text_kernel, side),
        in_specs=[SMEM, VMEM, VMEM, VMEM],
        out_specs=VMEM,
        out_shape=jax.ShapeDtypeStruct((half + 8 * side, width), jnp.float32),
        compiler_params=pltpu.CompilerParams(vmem_limit_bytes=16 * 2**20),
        cost_estimate=pl.CostEstimate(flops=5 * 10**8, bytes_accessed=4 * 10**6, transcendentals=0),
        name="text_products_%d" % side,
    )(place, rows, slopes, totals)


def finish_kernel(last, scale, unit, radius, accum, sums, grad, loss, scale_grad, bias_grad):
    values = unit[...]
    total = accum[...] * (scale[0] * last[0])
    grad[...] = (total - values * jnp.sum(values * total, -1, keepdims=True)) / radius[:, :1]
    loss[0] = sums[0, 0] * last[1]
    scale_grad[0] = sums[0, 1] * (scale[0] * last[1])
    bias_grad[0] = sums[0, 2] * last[1]


def finish(last, scale, unit, radius, accum, sums):
    one = jax.ShapeDtypeStruct((1,), jnp.float32)
    return pl.pallas_call(
        functools.partial(finish_kernel, last),
        in_specs=[SMEM, VMEM, VMEM, VMEM, VMEM],
        out_specs=[VMEM, SMEM, SMEM, SMEM],
        out_shape=[jax.ShapeDtypeStruct(unit.shape, jnp.float32), one, one, one],
        compiler_params=pltpu.CompilerParams(vmem_limit_bytes=8 * 2**20),
        cost_estimate=pl.CostEstimate(flops=10**6, bytes_accessed=10**6, transcendentals=0),
        name="finish",
    )(scale.reshape(1), unit, radius, accum, sums)


def swap_sum(blocks, stats, axis, unit):
    count, high, width = blocks.shape
    rider = jnp.concatenate(half_pieces(stats * (1 / unit)) + [jnp.zeros((high - 3, 128), jnp.float16)], 0)
    rider = jnp.broadcast_to(rider[None], (count, high, 128))
    got = swap(jnp.concatenate([blocks, rider], 2), axis)
    stats = jnp.sum(got[:, :3, width:].astype(jnp.float32), (0, 1)).reshape(1, 128) * unit
    return (jnp.sum(got[:, :, :width].astype(jnp.float32), 0), stats)


def half_pieces(value):
    pieces = []
    for _ in range(3):
        piece = lax.reduce_precision(value, 5, 10)
        pieces.append(piece.astype(jnp.float16))
        value = value - piece
    return pieces


def body(images, texts, image_ids, text_ids, log_scale, bias):
    width = images.shape[1]
    img_rows = images.shape[0]
    txt_rows = texts.shape[0]
    y, x, core = (lax.axis_index(a) for a in ("y", "x", "core"))
    z = lax.axis_index(Z)
    scale = jnp.exp(log_scale[0])
    copies, ux, rx = normalize(images, lax.axis_size("y"))
    uyb, uy, ry = normalize(texts, 1)

    own = swap(copies, "y").reshape(-1, width)
    cols = (uyb[0].astype(jnp.float32) * UNIT).astype(jnp.float16)
    own, cols = lax.optimization_barrier((own, cols))
    rows = spread(own, "x").reshape(-1, width)
    cols = lax.all_gather(cols, Z + ("core",), axis=0, tiled=True)
    cols = (cols.astype(jnp.float32) * (1 / UNIT)).astype(jnp.bfloat16)
    cols = cols.reshape(8, 2, txt_rows, width)
    mine = lax.dynamic_index_in_dim(cols, core, 1, keepdims=False)
    theirs = lax.dynamic_index_in_dim(cols, 1 - core, 1, keepdims=False)
    cols = jnp.concatenate([mine, theirs], 0).reshape(-1, width)

    col_ids = text_ids.reshape(8, 8, 4, 2, txt_rows)
    col_ids = lax.dynamic_index_in_dim(col_ids, y, 0, keepdims=False)
    col_ids = lax.dynamic_index_in_dim(col_ids, x, 1, keepdims=False)
    mine = lax.dynamic_index_in_dim(col_ids, core, 1, keepdims=False)
    theirs = lax.dynamic_index_in_dim(col_ids, 1 - core, 1, keepdims=False)
    col_ids = jnp.concatenate([mine, theirs], 0).reshape(1, -1).astype(jnp.float32)
    row_ids = image_ids.reshape(8, 8, 4, 2, img_rows)
    row_ids = lax.dynamic_index_in_dim(row_ids, z, 1, keepdims=False)
    row_ids = lax.dynamic_index_in_dim(row_ids, core, 2, keepdims=False)
    row_ids = row_ids.transpose(1, 0, 2).reshape(4, 1, -1)
    row_ids = jnp.concatenate([row_ids & -128, row_ids & 127, jnp.zeros((4, 6, 8 * img_rows), jnp.int32)], 1)
    row_ids = row_ids.astype(jnp.bfloat16)

    half = cols.shape[0] // 2
    high = rows.shape[0] // 4
    place = x.reshape(1).astype(jnp.int32)
    near, totals = slopes_of(place, jnp.stack([scale, bias[0]]), rows, cols, row_ids, col_ids)

    back = {}
    for k in (2, 1, 3, 0):
        drows = 64.0 * jnp.dot(near[k * high : (k + 1) * high], cols, preferred_element_type=jnp.float32)
        back[k] = drows.astype(jnp.float16) if k else drows

    got = shifted(text_products(1, place, rows, near, totals), "core", 1)
    mine = text_products(0, place, rows, near, totals)
    dcols = ((got[:half] + mine) * 32.0).astype(jnp.float16).reshape(8, txt_rows, width)
    dcols, back[1], back[2], back[3] = lax.optimization_barrier((dcols, back[1], back[2], back[3]))
    dcols, stats = swap_sum(dcols, got[half : half + 1, :128] + totals[:1, :128], Z, 128.0)
    stats = jnp.sum(spread(stats, "x"), 0)

    for k in (2, 1, 3):
        back[k] = shifted(back[k], "x", k)
    drows = sum(part.astype(jnp.float32) for part in back.values())
    drows = (drows * 0.25).astype(jnp.float16).reshape(8, -1, width)
    drows, stats = swap_sum(drows, stats, "y", 4096.0)
    text_grad = unnormalize(uy, ry[:, :1], scale * (dcols * (1 / 32.0)))
    image_grad, loss, scale_grad, bias_grad = finish(
        (0.0625, 1.0 / (txt_rows * 512)), scale, ux, rx, drows, stats
    )
    return (image_grad, text_grad, loss, scale_grad, bias_grad)


def solution(mesh):
    fine = Mesh(mesh.devices.reshape(SIZES), AXES)
    split = P(AXES, None)
    return jax.shard_map(
        body,
        mesh=fine,
        in_specs=(split, split, P(), P(), P(), P()),
        out_specs=(split, split, P(), P(), P()),
        check_vma=False,
    )
```

```python
import functools

import jax
import jax.numpy as jnp
from jax import lax
from jax.experimental import pallas as pl
from jax.experimental.pallas import tpu as pltpu
from jax.sharding import Mesh, PartitionSpec as P

AXES = ("y", "zh", "zl", "x", "core")
SIZES = (8, 2, 4, 4, 2)
Z = ("zh", "zl")
UNIT = 16384.0


VMEM = pl.BlockSpec(memory_space=pltpu.VMEM)
SMEM = pl.BlockSpec(memory_space=pltpu.SMEM)


def normalize_kernel(rows, copies, unit, radius):
    values = rows[...].astype(jnp.float32)
    length = jnp.sqrt(jnp.sum(values * values, -1, keepdims=True) + 1e-06)
    values = values / length
    unit[...] = values
    radius[...] = jnp.broadcast_to(length, radius.shape)
    for i in range(copies.shape[0]):
        copies[i] = values.astype(jnp.bfloat16)


def normalize(rows, count):
    shapes = ((count,) + rows.shape, rows.shape, (rows.shape[0], 128))
    whole = lambda shape: pl.BlockSpec(shape, lambda i: (0,) * len(shape))
    types = (jnp.bfloat16, jnp.float32, jnp.float32)
    return pl.pallas_call(
        normalize_kernel,
        grid=(1,),
        in_specs=[whole(rows.shape)],
        out_specs=[whole(shape) for shape in shapes],
        out_shape=[jax.ShapeDtypeStruct(*pair) for pair in zip(shapes, types)],
        compiler_params=pltpu.CompilerParams(vmem_limit_bytes=8 * 2**20),
        cost_estimate=pl.CostEstimate(flops=10**6, bytes_accessed=10**6, transcendentals=1000),
        name="normalize_%d" % count,
    )(rows)


def unnormalize(unit, radius, grad):
    return (grad - unit * jnp.sum(unit * grad, -1, keepdims=True)) / radius


def swap(value, axis):
    return lax.all_to_all(value, axis, 0, 0, tiled=False)


def shifted(value, axis, steps):
    count = lax.axis_size(axis)
    return lax.ppermute(value, axis, [(i, (i + steps) % count) for i in range(count)])


def spread(block, axis):
    count = lax.axis_size(axis)
    return swap(jnp.broadcast_to(block[None], (count,) + block.shape), axis)


def slopes_kernel(place, scalars, rows, cols, row_ids, col_ids, slopes, in_order, totals):
    parts = 4
    high = rows.shape[0] // parts
    sums = [0.0, 0.0, 0.0, 0.0]
    ones = jnp.ones((row_ids.shape[1], cols.shape[0]), jnp.bfloat16)
    for k in range(parts):
        part = pl.ds(pl.multiple_of(lax.rem(place[0] + k, parts) * high, high), high)
        dots = lax.dot_general(
            rows[part, :], cols[...], (((1,), (1,)), ((), ())), preferred_element_type=jnp.float32
        )
        logits = scalars[0] * dots + scalars[1]
        spot = lax.dot_general(
            row_ids[lax.rem(place[0] + k, parts)], ones, (((0,), (0,)), ((), ())), preferred_element_type=jnp.float32
        )
        match = spot == col_ids[...]
        against = jnp.where(match, -logits, logits)
        decay = jnp.exp(-jnp.abs(against))
        above = 1.0 + decay
        below = 1.0 / above
        weight = jnp.where(against >= 0.0, below, decay * below)
        objective = jnp.maximum(against, 0.0) + (decay - (above - 1.0)) * below
        product = above[:8]
        for i in range(1, high // 8):
            product = product * above[8 * i : 8 * (i + 1)]
        sums[3] += jnp.sum(jnp.log(product), 0, keepdims=True)
        slope = jnp.where(match, -weight, weight)
        slopes[k * high : (k + 1) * high, :] = slope.astype(jnp.bfloat16)
        in_order[part, :] = slope.astype(jnp.bfloat16)
        for i, term in enumerate((objective, slope * dots, slope)):
            sums[i] += jnp.sum(term, 0, keepdims=True)
    sums[0] += sums.pop()
    lane = lax.broadcasted_iota(jnp.int32, totals.shape, 1)
    total = jnp.zeros(totals.shape, jnp.float32)
    for i in range(3):
        total = jnp.where(lane == i, jnp.sum(sums[i], 1, keepdims=True), total)
    totals[...] = total


def text_kernel(side, place, rows, slopes, totals, out):
    half = slopes.shape[1] // 2
    out[:half, :] = lax.dot_general(
        slopes[:, side * half : (side + 1) * half],
        rows[...],
        (((0,), (0,)), ((), ())),
        preferred_element_type=jnp.float32,
    )
    if side:
        out[half:, :] = totals[...]


def slopes_of(place, scalars, rows, cols, row_ids, col_ids):
    wide, width = cols.shape
    return pl.pallas_call(
        slopes_kernel,
        in_specs=[SMEM, SMEM, VMEM, VMEM, VMEM, VMEM],
        out_specs=[VMEM, VMEM, VMEM],
        out_shape=(
            jax.ShapeDtypeStruct((rows.shape[0], wide), jnp.bfloat16),
            jax.ShapeDtypeStruct((rows.shape[0], wide), jnp.bfloat16),
            jax.ShapeDtypeStruct((8, width), jnp.float32),
        ),
        compiler_params=pltpu.CompilerParams(vmem_limit_bytes=20 * 2**20),
        cost_estimate=pl.CostEstimate(flops=10**9, bytes_accessed=4 * 10**6, transcendentals=10**6),
        name="slopes",
    )(place, scalars, rows, cols, row_ids, col_ids)


def text_products(side, place, rows, slopes, totals):
    half, width = slopes.shape[1] // 2, rows.shape[1]
    return pl.pallas_call(
        functools.partial(text_kernel, side),
        in_specs=[SMEM, VMEM, VMEM, VMEM],
        out_specs=VMEM,
        out_shape=jax.ShapeDtypeStruct((half + 8 * side, width), jnp.float32),
        compiler_params=pltpu.CompilerParams(vmem_limit_bytes=16 * 2**20),
        cost_estimate=pl.CostEstimate(flops=5 * 10**8, bytes_accessed=4 * 10**6, transcendentals=0),
        name="text_products_%d" % side,
    )(place, rows, slopes, totals)


def copies_kernel(block, out):
    for i in range(out.shape[0]):
        out[i] = block[...]


def copies_of(block, count):
    return pl.pallas_call(
        copies_kernel,
        in_specs=[VMEM],
        out_specs=VMEM,
        out_shape=jax.ShapeDtypeStruct((count,) + block.shape, block.dtype),
        compiler_params=pltpu.CompilerParams(vmem_limit_bytes=8 * 2**20),
        cost_estimate=pl.CostEstimate(flops=0, bytes_accessed=2 * 10**6, transcendentals=0),
        name="copies",
    )(block)


def finish_kernel(last, scale, unit, radius, accum, sums, grad, loss, scale_grad, bias_grad):
    values = unit[...]
    total = accum[...] * (scale[0] * last[0])
    grad[...] = (total - values * jnp.sum(values * total, -1, keepdims=True)) / radius[:, :1]
    loss[0] = sums[0, 0] * last[1]
    scale_grad[0] = sums[0, 1] * (scale[0] * last[1])
    bias_grad[0] = sums[0, 2] * last[1]


def finish(last, scale, unit, radius, accum, sums):
    one = jax.ShapeDtypeStruct((1,), jnp.float32)
    return pl.pallas_call(
        functools.partial(finish_kernel, last),
        in_specs=[SMEM, VMEM, VMEM, VMEM, VMEM],
        out_specs=[VMEM, SMEM, SMEM, SMEM],
        out_shape=[jax.ShapeDtypeStruct(unit.shape, jnp.float32), one, one, one],
        compiler_params=pltpu.CompilerParams(vmem_limit_bytes=8 * 2**20),
        cost_estimate=pl.CostEstimate(flops=10**6, bytes_accessed=10**6, transcendentals=0),
        name="finish",
    )(scale.reshape(1), unit, radius, accum, sums)


def swap_sum(blocks, stats, axis, unit):
    count, high, width = blocks.shape
    rider = jnp.concatenate(half_pieces(stats * (1 / unit)) + [jnp.zeros((high - 3, 128), jnp.float16)], 0)
    rider = jnp.broadcast_to(rider[None], (count, high, 128))
    got = swap(jnp.concatenate([blocks, rider], 2), axis)
    stats = jnp.sum(got[:, :3, width:].astype(jnp.float32), (0, 1)).reshape(1, 128) * unit
    return (jnp.sum(got[:, :, :width].astype(jnp.float32), 0), stats)


def half_pieces(value):
    pieces = []
    for _ in range(3):
        piece = lax.reduce_precision(value, 5, 10)
        pieces.append(piece.astype(jnp.float16))
        value = value - piece
    return pieces


def body(images, texts, image_ids, text_ids, log_scale, bias):
    width = images.shape[1]
    img_rows = images.shape[0]
    txt_rows = texts.shape[0]
    y, x, core = (lax.axis_index(a) for a in ("y", "x", "core"))
    z = lax.axis_index(Z)
    scale = jnp.exp(log_scale[0])
    copies, ux, rx = normalize(images, lax.axis_size("y"))
    uyb, uy, ry = normalize(texts, 1)

    own = swap(copies, "y").reshape(-1, width)
    cols = (uyb[0].astype(jnp.float32) * UNIT).astype(jnp.float16)
    own, cols = lax.optimization_barrier((own, cols))
    rows = swap(copies_of(own, lax.axis_size("x")), "x").reshape(-1, width)
    cols = lax.all_gather(cols, Z + ("core",), axis=0, tiled=True)
    cols = (cols.astype(jnp.float32) * (1 / UNIT)).astype(jnp.bfloat16)
    cols = cols.reshape(8, 2, txt_rows, width)
    mine = lax.dynamic_index_in_dim(cols, core, 1, keepdims=False)
    theirs = lax.dynamic_index_in_dim(cols, 1 - core, 1, keepdims=False)
    cols = jnp.concatenate([mine, theirs], 0).reshape(-1, width)

    col_ids = text_ids.reshape(8, 8, 4, 2, txt_rows)
    col_ids = lax.dynamic_index_in_dim(col_ids, y, 0, keepdims=False)
    col_ids = lax.dynamic_index_in_dim(col_ids, x, 1, keepdims=False)
    mine = lax.dynamic_index_in_dim(col_ids, core, 1, keepdims=False)
    theirs = lax.dynamic_index_in_dim(col_ids, 1 - core, 1, keepdims=False)
    col_ids = jnp.concatenate([mine, theirs], 0).reshape(1, -1).astype(jnp.float32)
    row_ids = image_ids.reshape(8, 8, 4, 2, img_rows)
    row_ids = lax.dynamic_index_in_dim(row_ids, z, 1, keepdims=False)
    row_ids = lax.dynamic_index_in_dim(row_ids, core, 2, keepdims=False)
    row_ids = row_ids.transpose(1, 0, 2).reshape(4, 1, -1)
    row_ids = jnp.concatenate([row_ids & -128, row_ids & 127, jnp.zeros((4, 6, 8 * img_rows), jnp.int32)], 1)
    row_ids = row_ids.astype(jnp.bfloat16)

    half = cols.shape[0] // 2
    high = rows.shape[0] // 4
    place = x.reshape(1).astype(jnp.int32)
    near, whole, totals = slopes_of(place, jnp.stack([scale, bias[0]]), rows, cols, row_ids, col_ids)

    back = {}
    for k in (2, 1, 3, 0):
        drows = 64.0 * jnp.dot(near[k * high : (k + 1) * high], cols, preferred_element_type=jnp.float32)
        back[k] = drows.astype(jnp.float16) if k else drows

    got = shifted(text_products(1, place, rows, whole, totals), "core", 1)
    mine = text_products(0, place, rows, whole, totals)
    dcols = ((got[:half] + mine) * 32.0).astype(jnp.float16).reshape(8, txt_rows, width)
    dcols, back[1], back[2], back[3] = lax.optimization_barrier((dcols, back[1], back[2], back[3]))
    dcols, stats = swap_sum(dcols, got[half : half + 1, :128] + totals[:1, :128], Z, 128.0)
    stats = jnp.sum(spread(stats, "x"), 0)

    for k in (2, 1, 3):
        back[k] = shifted(back[k], "x", k)
    drows = sum(part.astype(jnp.float32) for part in back.values())
    drows = (drows * 0.25).astype(jnp.float16).reshape(8, -1, width)
    drows, stats = swap_sum(drows, stats, "y", 4096.0)
    text_grad = unnormalize(uy, ry[:, :1], scale * (dcols * (1 / 32.0)))
    image_grad, loss, scale_grad, bias_grad = finish(
        (0.0625, 1.0 / (txt_rows * 512)), scale, ux, rx, drows, stats
    )
    return (image_grad, text_grad, loss, scale_grad, bias_grad)


def solution(mesh):
    fine = Mesh(mesh.devices.reshape(SIZES), AXES)
    split = P(AXES, None)
    return jax.shard_map(
        body,
        mesh=fine,
        in_specs=(split, split, P(), P(), P(), P()),
        out_specs=(split, split, P(), P(), P()),
        check_vma=False,
    )
```
